256 devices in a mesh: fsdp: 4 (over x), expert: 8 (over z), tensor: 8 (over y, core).
Axes of the slice: x: 4, y: 4, z: 8, core: 2. Of those that a mesh axis runs over, the one named last changes fastest.
Arguments:
- tokens: bfloat16 [2, 512, 4096], P(None, 'expert'), may hold values from -6 to 6
- route: int32 [2, 512, 2], P(None, 'expert'), may hold values from 0 to 7, all different within a row; in each aligned block of 64 rows (0 to 63, 64 to 127, ..., all dimensions but the last counted through in order) at most 32 rows name the same one
- route_weight: float32 [2, 512, 2], P(None, 'expert'), may hold values from 0.1 to 1
- gate_up: bfloat16 [8, 2, 4096, 8192], P('expert', None, None, ('fsdp', 'tensor')), may hold values from -0.09375 to 0.09375
- down_weight: bfloat16 [8, 8192, 4096], P('expert', ('fsdp', 'tensor')), may hold values from -0.125 to 0.125
- adam_first: float32 [8, 2048, 4096], P(None, ('fsdp', 'tensor'), 'expert'), may hold values from -2.5 to 2.5
- adam_second: float32 [8, 2048, 4096], P(None, ('fsdp', 'tensor'), 'expert'), may hold values from 0.05 to 1
- gradient: bfloat16 [8, 2048, 4096], P(None, ('fsdp', 'tensor'), 'expert'), may hold values from -6 to 6
- block_list: int32 [8, 32, 4], P(None, ('fsdp', 'tensor')), may hold values from 0 to 7, as said below
- block_count: int32 [8, 32], P(None, ('fsdp', 'tensor')), may hold values from 1 to 4, as said below
Outputs:
- mixed: bfloat16 [2, 512, 4096], P(None, 'expert', ('fsdp', 'tensor'))
- first_new: float32 [8, 2048, 4096], P(None, ('fsdp', 'tensor'), 'expert')
- second_new: float32 [8, 2048, 4096], P(None, ('fsdp', 'tensor'), 'expert')
The draws below stay inside these ranges and needn't reach their ends.
Inputs may be any that keep to these rules, and one draw needn't show every extreme that they name: `route`: the two experts of a token differ; in each aligned block of 64 tokens of one step no expert is named more than 32 times. `block_list`: the 4 entries of one list are distinct block numbers; only the first block_count entries are applied. `block_count`: 4 is reached in every draw.
All inputs are finite; a program needn't handle non-finite values.
Results may differ from the reference program's by a relative error of at most 0.023.
Values may be sent and summed in bfloat16 or wider, within the bound.
A program may use at most 64 MiB of HBM per device.

```python
import math
import jax
import jax.numpy as jnp
import numpy as np
from jax import lax

D = 4096
HID = 8192
E = 8
STRIDE = 4
BLOCK_ROWS = 8
MAXCH = 4
S = 2
TOK_DEV = 64
TOK = 512
CAP = 32
SHARDS = 32
HSHARD = 256
BUCKET = 2048
NBLOCKS = 8
N_EXPERT = 8


def draw_block_list(key, part):
    key = jax.random.fold_in(key, 7)
    row_keys = jax.random.split(key, E * SHARDS)
    orders = jax.vmap(lambda row_key: jax.random.permutation(row_key, NBLOCKS))(row_keys)
    return orders[:, :MAXCH].reshape(E, SHARDS, MAXCH).astype(jnp.int32)


def draw_block_count(key, part):
    key = jax.random.fold_in(key, 13)
    key_base, key_busy, key_top = jax.random.split(key, 3)
    base_count = 1 + (jax.random.randint(key_base, (E, SHARDS), 0, 4) == 0).astype(jnp.int32)
    busy_flag = jax.random.randint(key_busy, (E, SHARDS), 0, 16) == 0
    counts = jnp.where(busy_flag, MAXCH, base_count)
    top_index = jax.random.randint(key_top, (), 0, E * SHARDS)
    flat_counts = counts.reshape(-1).at[top_index].set(MAXCH)
    return flat_counts.reshape(E, SHARDS).astype(jnp.int32)


def with_spikes(drawn, rng, source, target, parts, factor):
    owner, partner = [(jnp.arange(drawn.shape[position]) // (drawn.shape[position] // parts)).reshape([-1 if axis == position else 1 for axis in range(drawn.ndim)]) for position in (source, target)]
    chosen = jax.random.permutation(rng, parts)[partner]
    strong = (owner == chosen) | (owner == (partner + parts // 2) % parts)
    return jnp.where(strong, factor * drawn, drawn)


def block_scale(stream_key, dims, cuts, least, top_value):
    loudness = 1.0
    for axis_at, shards_of in cuts:
        draws = jax.random.uniform(jax.random.fold_in(jax.random.fold_in(stream_key, 6), axis_at), (shards_of,), jnp.float32, least / len(cuts), top_value / len(cuts))
        loudness = loudness * jnp.repeat(jnp.exp(draws), dims[axis_at] // shards_of).reshape((-1,) + (1,) * (len(dims) - 1 - axis_at))
    return loudness


def assign_block(key, own, number, rows, number_of, top, bound, slope):
    sequence = jax.random.permutation(key, number_of)
    heavy_load, ordinary = portions_of(number_of, rows * top, bound, slope, True), portions_of(number_of, rows * top, bound, slope, False)
    places = jnp.arange(number_of)

    def named(sizes, rotation):
        used = int((sizes > 0).sum())
        fixed = max(1, used // 4)
        moved = fixed + (places - fixed + rotation * (used - fixed)) % max(1, number_of - fixed)
        return jnp.zeros((number_of,), jnp.int32).at[sequence[jnp.where(places < fixed, places, moved)]].set(jnp.asarray(sizes, jnp.int32))

    sizes = jnp.where(number % 4 == 0, named(heavy_load, number // 4), named(ordinary, number - number // 4 - 1))
    mixed = jax.random.permutation(jax.random.fold_in(own, 3), number_of)
    donor, taker = mixed[0:number_of // 2 * 2:2], mixed[1:number_of // 2 * 2:2]
    room = jnp.minimum(sizes[donor] - 1, bound - sizes[taker]) // 2
    room = jnp.where((donor == sequence[0]) | (taker == sequence[0]) | (sizes[taker] == 0), 0, jnp.maximum(room, 0))
    moved = jax.random.randint(jax.random.fold_in(own, 4), (number_of // 2,), 0, 1 << 20) % (room + 1)
    sizes = sizes.at[donor].add(-moved).at[taker].add(moved)
    members = jnp.searchsorted(jnp.cumsum(sizes), jnp.arange(rows * top), side="right").astype(jnp.int32)
    table = members.reshape(top, rows).T
    table = table[jax.random.permutation(jax.random.fold_in(own, 1), rows)]
    rotation = jax.random.randint(jax.random.fold_in(own, 2), (rows, 1), 0, top)
    return jnp.take_along_axis(table, (jnp.arange(top)[None, :] + rotation) % top, axis=1)


def portions_of(count, total, bound, lean, full):
    weights = [(1 << 20) // math.isqrt(standing ** lean) + 1 for standing in range(1, count + 1)]
    largest = bound if full else min(bound, max(-(-total // count), total * weights[0] // sum(weights)))
    least = 1 if total - largest >= count - 1 else 0
    given, spare = [largest] + [least] * (count - 1), total - largest - least * (count - 1)
    while spare > 0:
        free = [i for i in range(1, count) if given[i] < largest] or [i for i in range(1, count) if given[i] < bound]
        pool, left = sum([weights[i] for i in free]), spare
        for i in free:
            more = min(bound - given[i], max(1, left * weights[i] // pool), spare)
            given[i] = given[i] + more
            spare = spare - more
    return np.array(given)


def bell_draw(rng, extent, deviation, limit, cuts=(), kind=jnp.bfloat16):
    entries = deviation * jax.random.normal(rng, extent, jnp.float32)
    if cuts:
        entries = entries * block_scale(rng, extent, cuts, -0.22, 0.18)
    return jnp.clip(entries, -limit, limit).astype(kind)


def noise_with(stream_key, shape, scale, most, shards, heavy, dtype=jnp.bfloat16):
    values = scale * jax.random.normal(stream_key, shape, jnp.float32)
    if shards:
        values = values * block_scale(stream_key, shape, shards, -0.22, 0.18)
    return jnp.clip(with_spikes(values, jax.random.fold_in(stream_key, 3), *heavy), -most, most).astype(dtype)


def setup_inputs(seed: int = 0) -> dict:
    seeds = jax.random.split(jax.random.key(seed), 11)
    tokens = bell_draw(seeds[0], (S, TOK, D), 1.0, 6.0, ((1, 8),))
    route_keys = jax.random.split(jax.random.fold_in(seeds[1], 1), S * TOK // TOK_DEV)
    route_turns = jax.random.permutation(jax.random.fold_in(seeds[1], 3), S * TOK // TOK_DEV)
    route = jax.vmap(lambda own, number: assign_block(jax.random.fold_in(seeds[1], 2), own, number, TOK_DEV, E, 2, TOK_DEV // 2, 2))(route_keys, route_turns).reshape((S, TOK, 2))
    route_weight = jnp.clip(0.1 + 0.9 * jax.random.uniform(seeds[2], (S, TOK, 2), jnp.float32) ** block_scale(seeds[2], (S, TOK, 2), ((1, 8),), -0.2, 0.2), 0.1, 1.0)
    gate_up = bell_draw(seeds[3], (E, 2, D, HID), D ** -0.5, 0.09375, ((0, 8), (3, 32)))
    down_weight = noise_with(seeds[4], (E, HID, D), HID ** -0.5, 0.125, ((0, 8), (1, 32)), (1, 2, 32, 2.75))
    adam_first = bell_draw(seeds[5], (E, BUCKET, D), 0.3, 2.5, ((1, 32), (2, 8)), jnp.float32)
    adam_second = jnp.clip(jnp.exp(math.log(1.0) - 2.9957323 * jax.random.uniform(seeds[6], (E, BUCKET, D), jnp.float32) ** block_scale(seeds[6], (E, BUCKET, D), ((1, 32), (2, 8)), -0.2, 0.2)), 0.05, 1.0)
    gradient = bell_draw(seeds[7], (E, BUCKET, D), 1.0, 6.0, ((1, 32), (2, 8)))
    block_list = draw_block_list(jax.random.fold_in(seeds[10], 71), 0)
    block_count = draw_block_count(jax.random.fold_in(seeds[10], 71), 0)
    return {"tokens": tokens, "route": route, "route_weight": route_weight, "gate_up": gate_up, "down_weight": down_weight, "adam_first": adam_first, "adam_second": adam_second, "gradient": gradient, "block_list": block_list, "block_count": block_count}


BETA_ONE = 0.9
BETA_TWO = 0.95
LEARN_RATE = 0.03
ADAM_EPS = 1e-08
FIRST_FIX = 1.0 - 0.9 ** 10
SECOND_FIX = 1.0 - 0.95 ** 10

def adam_moments(adam_first, adam_second, gradient):
    grad_wide = gradient.astype(jnp.float32)
    first_new = BETA_ONE * adam_first + (1.0 - BETA_ONE) * grad_wide
    second_new = BETA_TWO * adam_second + (1.0 - BETA_TWO) * grad_wide * grad_wide
    step_size = LEARN_RATE * (first_new / FIRST_FIX) / (jnp.sqrt(second_new / SECOND_FIX) + ADAM_EPS)
    return (first_new, second_new, (-step_size).astype(jnp.bfloat16))

def updated_down(down_weight, delta, block_list, block_count):
    listed = jnp.arange(MAXCH)[None, None, :] < block_count[:, :, None]
    marked = jnp.any((block_list[:, :, :, None] == jnp.arange(NBLOCKS)[None, None, None, :]) & listed[:, :, :, None], axis=2)
    row_mask = jnp.repeat(marked.reshape(E, SHARDS * NBLOCKS), BLOCK_ROWS, axis=1)
    strided = down_weight.reshape(E, BUCKET, STRIDE, D)
    fresh_rows = (strided[:, :, 0, :].astype(jnp.float32) + jnp.where(row_mask[:, :, None], delta.astype(jnp.float32), 0.0)).astype(jnp.bfloat16)
    return jnp.concatenate([fresh_rows[:, :, None, :], strided[:, :, 1:, :]], axis=2).reshape(E, HID, D)

def expert_rows(token_rows, gate_weights, down_rows):
    gate_value = jnp.dot(token_rows, gate_weights[0], preferred_element_type=jnp.float32)
    up_value = jnp.dot(token_rows, gate_weights[1], preferred_element_type=jnp.float32)
    hidden = (jax.nn.silu(gate_value) * up_value).astype(jnp.bfloat16)

    def add_shard(shard_index, running):
        first_unit = (shard_index * HSHARD).astype(jnp.int32)
        shard_term = jnp.dot(lax.dynamic_slice_in_dim(hidden, first_unit, HSHARD, 1), lax.dynamic_slice_in_dim(down_rows, first_unit, HSHARD, 0), preferred_element_type=jnp.float32)
        rounded = lax.optimization_barrier(shard_term.astype(jnp.bfloat16))
        return running + rounded.astype(jnp.float32)
    return lax.fori_loop(0, SHARDS, add_shard, jnp.zeros((token_rows.shape[0], D), jnp.float32))

def reference(tokens, route, route_weight, gate_up, down_weight, adam_first, adam_second, gradient, block_list, block_count):
    first_new, second_new, delta = adam_moments(adam_first, adam_second, gradient)
    down_new = updated_down(down_weight, delta, block_list, block_count)
    flat_tokens = tokens.reshape(S * TOK, D)
    flat_route = route.reshape(-1)
    flat_weight = route_weight.reshape(-1)
    owner_token = (jnp.arange(S * TOK * 2) // 2).astype(jnp.int32)
    capacity_all = S * N_EXPERT * CAP
    combined = jnp.zeros((S * TOK, D), jnp.float32)
    for expert in range(E):
        chosen = flat_route == expert
        picked = jnp.nonzero(chosen, size=capacity_all, fill_value=0)[0].astype(jnp.int32)
        live_slot = jnp.arange(capacity_all) < jnp.sum(chosen.astype(jnp.int32))
        token_index = owner_token[picked]
        result = expert_rows(flat_tokens[token_index], gate_up[expert], down_new[expert])
        pair_weight = jnp.where(live_slot, flat_weight[picked], 0.0)
        combined = combined.at[token_index].add(pair_weight[:, None] * result)
    return (combined.reshape(S, TOK, D).astype(jnp.bfloat16), first_new, second_new)
```

```python
import jax
import jax.numpy as jnp
from jax import lax
from jax.experimental import pallas as pl
from jax.experimental.pallas import tpu as pltpu
from jax.sharding import PartitionSpec as P

F32 = jnp.float32
BF16 = jnp.bfloat16
MESH_ID = pl.DeviceIdType.MESH

E = 8
BLOCK_ROWS = 8
MAXCH = 4
CAP = 32
TOK = 64
D = 4096
HS = 256
SLOTS = E * CAP
QUART = 512
LANE = 128
KDOWN = 2 * HS + 128
PIECE = 128

BETA_ONE = 0.9
BETA_TWO = 0.95
LEARN_RATE = 0.03
ADAM_EPS = 1e-08
FIRST_FIX = 1.0 - 0.9**10
SECOND_FIX = 1.0 - 0.95**10


def adam_kernel(list_ref, m_ref, v_ref, g_ref, first_ref, second_ref, delta_ref):
    e = pl.program_id(0)
    grad = g_ref[0].astype(F32)
    first_ref[0] = BETA_ONE * m_ref[0] + (1.0 - BETA_ONE) * grad
    second_ref[0] = BETA_TWO * v_ref[0] + (1.0 - BETA_TWO) * grad * grad
    parts = []
    for j in range(MAXCH):
        rows = pl.ds(pl.multiple_of(list_ref[j, e] * BLOCK_ROWS, BLOCK_ROWS), BLOCK_ROWS)
        top = first_ref[0, rows, :] / FIRST_FIX
        parts.append(
            -(LEARN_RATE * top / (jnp.sqrt(second_ref[0, rows, :] / SECOND_FIX) + ADAM_EPS))
        )
    delta_ref[0] = jnp.concatenate(parts, axis=0).astype(BF16)


def adam(block_list, adam_first, adam_second, gradient):
    rows, cols = adam_first.shape[1:]
    spec = pl.BlockSpec((1, rows, cols), lambda e: (e, 0, 0))
    return pl.pallas_call(
        adam_kernel,
        grid=(E,),
        in_specs=[pl.BlockSpec(memory_space=pltpu.SMEM), spec, spec, spec],
        out_specs=[
            spec,
            spec,
            pl.BlockSpec((1, MAXCH * BLOCK_ROWS, cols), lambda e: (e, 0, 0)),
        ],
        out_shape=[
            jax.ShapeDtypeStruct((E, rows, cols), F32),
            jax.ShapeDtypeStruct((E, rows, cols), F32),
            jax.ShapeDtypeStruct((E, MAXCH * BLOCK_ROWS, cols), BF16),
        ],
        name="adam",
    )(block_list, adam_first, adam_second, gradient)


def tri(j):
    return lax.rem(j * (j + 1) // 2, 4)


def expert_kernel(
    route_ref,
    weight_ref,
    list_ref,
    count_ref,
    tokens,
    gate_up,
    down,
    delta,
    out_ref,
    tok,
    zsend,
    xbuf,
    gu,
    dn,
    acc,
    hid,
    mix,
    tgt,
    r1send,
    r1recv,
    r1own,
    r2send,
    r2recv,
    r2own,
    r3buf,
    back,
    load_sem,
    gu_sem,
    sib_send,
    sib_recv,
    z_send,
    z_recv,
    f_send,
    f_recv,
    d_send,
    d_recv,
    m_send,
    m_recv,
    r1s,
    r1r,
    r2s,
    r2r,
    r3s,
    r3r,
):
    x = lax.axis_index("fsdp")
    z = lax.axis_index("expert")
    t = lax.axis_index("tensor")
    y = t // 2
    c = lax.rem(t, 2)

    def at(i, j, k, core):
        return (lax.rem(x + i, 4), lax.rem(z + k, 8), lax.rem(y + j, 4) * 2 + core)

    def remote(src, dst, ssem, rsem, where):
        return pltpu.make_async_remote_copy(
            src_ref=src,
            dst_ref=dst,
            send_sem=ssem,
            recv_sem=rsem,
            device_id=where,
            device_id_type=MESH_ID,
        )

    barrier = pltpu.get_barrier_semaphore()
    sibling = at(0, 0, 0, 1 - c)
    for i in range(1, 4):
        for where in (at(i, 0, 0, c), at(0, i, 0, c)):
            pl.semaphore_signal(barrier, inc=1, device_id=where, device_id_type=MESH_ID)
    for k in range(8):
        pl.semaphore_signal(
            barrier, inc=1, device_id=at(0, 0, k, 1 - c), device_id_type=MESH_ID
        )
        if k:
            pl.semaphore_signal(
                barrier, inc=1, device_id=at(0, 0, k, c), device_id_type=MESH_ID
            )

    tok_loads = [
        pltpu.make_async_copy(
            tokens.at[c, :, pl.ds(pl.multiple_of(col, QUART), QUART)], tok.at[h], load_sem.at[h]
        )
        for h, col in enumerate((x * QUART, 2048 + y * QUART))
    ]
    for cp in tok_loads:
        cp.start()

    def chunk_rows(h, i):
        own = x + h * (y - x)
        start = h * 2048 + lax.rem(own - i + 4, 4) * QUART
        return pl.ds(pl.multiple_of(start, QUART), QUART)

    def gu_load(q):
        rows = chunk_rows(lax.rem(q, 2), tri(q // 2))
        return pltpu.make_async_copy(
            gate_up.at[:, rows, :], gu.at[0, :, rows, :], gu_sem.at[q]
        )

    @pl.loop(0, 8)
    def _(q):
        gu_load(q).start()

    down_load = pltpu.make_async_copy(down, dn.at[pl.ds(0, HS)], load_sem.at[2])
    down_load.start()
    delta_cols = pl.ds(pl.multiple_of(z * QUART, QUART), QUART)
    delta_load = pltpu.make_async_copy(
        delta.at[z], dn.at[pl.ds(2 * HS, CAP), delta_cols], load_sem.at[3]
    )
    delta_load.start()

    lower = (
        lax.broadcasted_iota(jnp.int32, (TOK, TOK), 0)
        < lax.broadcasted_iota(jnp.int32, (TOK, TOK), 1)
    ).astype(BF16)
    expert_ids = lax.broadcasted_iota(jnp.int32, (E, TOK), 0)
    slot_ids = lax.broadcasted_iota(jnp.int32, (CAP, TOK), 0).astype(F32)

    def slots_of(step):
        named = route_ref[step]
        hits = [named[k : k + 1, :] == expert_ids for k in range(2)]
        any_hit = jnp.where(hits[0] | hits[1], 1.0, 0.0)
        place = jnp.dot(any_hit.astype(BF16), lower, preferred_element_type=F32)
        place = jnp.where(any_hit > 0.5, place, -1.0)
        return hits, [slot_ids == place[e : e + 1, :] for e in range(E)]

    _, chosen = slots_of(c)
    selector = jnp.concatenate([jnp.where(m, 1.0, 0.0) for m in chosen], axis=0).astype(BF16)
    for h in range(2):
        tok_loads[h].wait()
        zsend[h] = jnp.dot(selector, tok[h], preferred_element_type=F32).astype(BF16)
    own_rows = pl.ds(pl.multiple_of(z * CAP, CAP), CAP)
    for h in range(2):
        xbuf[h, 0, own_rows, :] = zsend[h, own_rows, :]

    pl.semaphore_wait(barrier, 21)

    def z_copy(h, k):
        e = lax.rem(z + k, 8)
        rows = pl.ds(pl.multiple_of(e * CAP, CAP), CAP)
        return remote(
            zsend.at[h, rows, :],
            xbuf.at[h, 0, own_rows, :],
            z_send.at[h, k],
            z_recv.at[h, k],
            at(0, 0, k, c),
        )

    for k in (4, 3, 5, 2, 6, 1, 7):
        for h in range(2):
            z_copy(h, k).start()

    def forward(h, i, k):
        rows = pl.ds(pl.multiple_of(lax.rem(z - k + 8, 8) * CAP, CAP), CAP)
        return remote(
            xbuf.at[h, 0, rows, :],
            xbuf.at[h, i, rows, :],
            f_send.at[h, i],
            f_recv.at[h, i],
            at(i * (1 - h), i * h, 0, c),
        )

    def forward_all(h, i):
        return remote(
            xbuf.at[h, 0],
            xbuf.at[h, i],
            f_send.at[h, i],
            f_recv.at[h, i],
            at(i * (1 - h), i * h, 0, c),
        )

    for i in (2, 1, 3):
        for h in range(2):
            forward(h, i, 0).start()

    def gu_swap(q):
        rows = chunk_rows(lax.rem(q, 2), tri(q // 2))
        return remote(
            gate_up.at[:, rows, :],
            gu.at[1, :, rows, :],
            sib_send.at[q],
            sib_recv.at[q],
            sibling,
        )

    @pl.loop(0, 8)
    def _(q):
        gu_swap(q).start()

    def d_copy(k):
        e = lax.rem(z + k, 8)
        return remote(
            delta.at[e],
            dn.at[pl.ds(2 * HS, CAP), delta_cols],
            d_send.at[k],
            d_recv.at[k],
            at(0, 0, k, c),
        )

    for k in (4, 3, 5, 2, 6, 1, 7):
        d_copy(k).start()

    down_swap = remote(
        down, dn.at[pl.ds(HS, HS)], m_send.at[0], m_recv.at[0], sibling
    )
    down_swap.start()

    here = lax.broadcasted_iota(jnp.int32, (MAXCH, E), 1) == z
    blocks = jnp.sum(jnp.where(here, list_ref[...], 0), axis=1, keepdims=True)
    count = jnp.sum(jnp.where(here[0:1], count_ref[...], 0), axis=1, keepdims=True)
    lane = lax.broadcasted_iota(jnp.int32, (8, LANE), 1)

    def targets(first_lane, first_unit):
        units = jnp.full((8, LANE), -1, jnp.int32)
        for j in range(MAXCH):
            start = first_lane + BLOCK_ROWS * j
            live = (lane >= start) & (lane < start + BLOCK_ROWS) & (count > j)
            unit = first_unit + 4 * (BLOCK_ROWS * blocks[j : j + 1, :] + lane - start)
            units = jnp.where(live, unit, units)
        return units.astype(F32)

    tgt[0] = targets(0, 0)
    tgt[1] = targets(CAP, HS)
    target_swap = remote(tgt.at[1], tgt.at[2], m_send.at[1], m_recv.at[1], sibling)
    target_swap.start()
    dn[pl.ds(2 * HS + 2 * CAP, 2 * CAP), :] = jnp.zeros((2 * CAP, D), BF16)

    for k in (1, 7, 2, 6, 3, 5, 4):
        for h in range(2):
            z_copy(h, k).wait_recv()
            for i in (2, 1, 3):
                forward(h, i, k).start()

    for step in range(2):
        hits, chosen = slots_of(step)
        w = weight_ref[step]
        by_expert = jnp.where(hits[0], w[0:1, :], 0.0) + jnp.where(hits[1], w[1:2, :], 0.0)
        full = jnp.concatenate(
            [jnp.where(chosen[e], by_expert[e : e + 1, :], 0.0) for e in range(E)], axis=0
        )
        full = full.T
        high = full.astype(BF16)
        mix[step, pl.ds(0, TOK), :] = high
        mix[step, pl.ds(TOK, TOK), :] = (full - high.astype(F32)).astype(BF16)

    def project(q, first):
        h, i = lax.rem(q, 2), tri(q // 2)
        gu_load(q).wait()
        gu_swap(q).wait_recv()
        rows = chunk_rows(h, i)
        block = xbuf[h, i]
        for s in range(2):
            for g in range(2):
                term = jnp.dot(block, gu[s, g, rows, :], preferred_element_type=F32)
                if first:
                    acc[2 * s + g] = term
                else:
                    acc[2 * s + g] += term

    project(0, True)

    @pl.loop(1, 2)
    def _(q):
        project(q, False)

    @pl.loop(2, 8)
    def _(q):
        forward_all(lax.rem(q, 2), tri(q // 2)).wait_recv()
        project(q, False)

    delta_load.wait()
    for k in range(1, 8):
        d_copy(k).wait_recv()
    delta_swap = remote(
        dn.at[pl.ds(2 * HS, CAP)],
        dn.at[pl.ds(2 * HS + CAP, CAP)],
        m_send.at[2],
        m_recv.at[2],
        sibling,
    )
    delta_swap.start()

    for s in range(2):
        gate = acc[2 * s]
        hid[:, pl.ds(s * HS, HS)] = (jax.nn.silu(gate) * acc[2 * s + 1]).astype(BF16)
    target_swap.wait_recv()
    unit = jnp.where(lane < CAP, tgt[0], tgt[2])[0:1, :]
    picks = (
        lax.broadcasted_iota(jnp.int32, (2 * HS, LANE), 0).astype(F32) == unit
    ).astype(BF16)
    hid[:, pl.ds(2 * HS, LANE)] = jnp.dot(
        hid[:, pl.ds(0, 2 * HS)], picks, preferred_element_type=F32
    ).astype(BF16)

    down_load.wait()
    down_swap.wait_recv()
    delta_swap.wait_recv()

    def down_term(h, i):
        cols = []
        for j in range(4):
            a, b = i + h * (j - i), j + h * (i - j)
            block = 8 * lax.rem(x + a, 4) + 2 * lax.rem(y + b, 4) + h
            cols.append(dn[:, pl.ds(pl.multiple_of(block * LANE, LANE), LANE)])
        return jnp.dot(hid[...], jnp.concatenate(cols, axis=1), preferred_element_type=F32)

    def r1_copy(h, i, p):
        rows = pl.ds(p * PIECE, PIECE)
        return remote(
            r1send.at[h, i - 1, rows, :],
            r1recv.at[h, i - 1, rows, :],
            r1s.at[h, i - 1, p],
            r1r.at[h, i - 1, p],
            at(i * (1 - h), i * h, 0, c),
        )

    @pl.loop(0, 6)
    def _(q):
        h, i = lax.rem(q, 2), lax.rem(6 - tri(q // 2), 4)
        r1send[h, i - 1] = down_term(h, i).astype(BF16)
        for p in range(2):
            r1_copy(h, i, p).start()

    @pl.loop(0, 2)
    def _(h):
        r1own[h] = down_term(h, 0)

    def r2_copy(h, j, p):
        rows = pl.ds(p * PIECE, PIECE)
        return remote(
            r2send.at[h, j - 1, rows, :],
            r2recv.at[h, j - 1, rows, :],
            r2s.at[h, j - 1, p],
            r2r.at[h, j - 1, p],
            at(j * h, j * (1 - h), 0, c),
        )

    for p in range(2):
        rows = pl.ds(p * PIECE, PIECE)
        for h in range(2):
            for i in (1, 3, 2):
                r1_copy(h, i, p).wait_recv()
            for j in (2, 1, 3, 0):
                cols = pl.ds(j * LANE, LANE)
                total = r1own[h, rows, cols]
                for i in range(3):
                    total += r1recv[h, i, rows, cols].astype(F32)
                if j:
                    r2send[h, j - 1, rows, :] = total.astype(BF16)
                    r2_copy(h, j, p).start()
                else:
                    r2own[h, rows, :] = total

    def r3_copy(h, e):
        rows = pl.ds(pl.multiple_of(e * CAP, CAP), CAP)
        return remote(
            r3buf.at[h, rows, :],
            back.at[c, own_rows, :],
            r3s.at[e, h],
            r3r.at[z, c],
            (x, e, y * 2 + h),
        )

    def r3_wait(step, e):
        rows = pl.ds(pl.multiple_of(e * CAP, CAP), CAP)
        remote(
            r3buf.at[step, rows, :],
            back.at[step, rows, :],
            r3s.at[e, step],
            r3r.at[e, step],
            (x, e, y * 2 + step),
        ).wait_recv()

    def not_self(e, core):
        return jnp.logical_or(e != z, core != c)

    for p in range(2):
        rows = pl.ds(p * PIECE, PIECE)
        for h in range(2):
            for j in (1, 3, 2):
                r2_copy(h, j, p).wait_recv()
            total = r2own[h, rows, :]
            for j in range(3):
                total += r2recv[h, j, rows, :].astype(F32)
            r3buf[h, rows, :] = total.astype(BF16)
            for e in range(4 * p, 4 * p + 4):

                @pl.when(not_self(e, h))
                def _(h=h, e=e):
                    r3_copy(h, e).start()

    back[c, own_rows, :] = r3buf[c, own_rows, :]
    for step in range(2):
        for e in range(E):

            @pl.when(not_self(e, step))
            def _(step=step, e=e):
                r3_wait(step, e)

        both = jnp.dot(mix[step], back[step], preferred_element_type=F32)
        out_ref[step] = (both[:TOK] + both[TOK:]).astype(BF16)

    for h in range(2):
        for k in range(1, 8):
            z_copy(h, k).wait_send()
        for i in range(1, 4):
            forward_all(h, i).wait_send()
            for p in range(2):
                r1_copy(h, i, p).wait_send()
                r2_copy(h, i, p).wait_send()
        for e in range(E):

            @pl.when(not_self(e, h))
            def _(h=h, e=e):
                r3_copy(h, e).wait_send()

    @pl.loop(0, 8)
    def _(q):
        gu_swap(q).wait_send()

    for k in range(1, 8):
        d_copy(k).wait_send()
    for cp in (down_swap, target_swap, delta_swap):
        cp.wait_send()


def expert_layer(route, weight, block_list, block_count, tokens, gate_up, down, delta):
    vmem = pl.BlockSpec(memory_space=pltpu.VMEM)
    hbm = pl.BlockSpec(memory_space=pl.ANY)
    dma = pltpu.SemaphoreType.DMA
    return pl.pallas_call(
        expert_kernel,
        in_specs=[vmem] * 4 + [hbm] * 4,
        out_specs=vmem,
        out_shape=jax.ShapeDtypeStruct((2, TOK, LANE), BF16),
        scratch_shapes=[
            pltpu.VMEM((2, TOK, QUART), BF16),
            pltpu.VMEM((2, SLOTS, QUART), BF16),
            pltpu.VMEM((2, 4, SLOTS, QUART), BF16),
            pltpu.VMEM((2, 2, D, HS), BF16),
            pltpu.VMEM((KDOWN, D), BF16),
            pltpu.VMEM((4, SLOTS, HS), F32),
            pltpu.VMEM((SLOTS, KDOWN), BF16),
            pltpu.VMEM((2, 2 * TOK, SLOTS), BF16),
            pltpu.VMEM((3, 8, LANE), F32),
            pltpu.VMEM((2, 3, SLOTS, QUART), BF16),
            pltpu.VMEM((2, 3, SLOTS, QUART), BF16),
            pltpu.VMEM((2, SLOTS, QUART), F32),
            pltpu.VMEM((2, 3, SLOTS, LANE), BF16),
            pltpu.VMEM((2, 3, SLOTS, LANE), BF16),
            pltpu.VMEM((2, SLOTS, LANE), F32),
            pltpu.VMEM((2, SLOTS, LANE), BF16),
            pltpu.VMEM((2, SLOTS, LANE), BF16),
            dma((4,)),
            dma((8,)),
            dma((8,)),
            dma((8,)),
            dma((2, 8)),
            dma((2, 8)),
            dma((2, 4)),
            dma((2, 4)),
            dma((8,)),
            dma((8,)),
            dma((3,)),
            dma((3,)),
            dma((2, 3, 2)),
            dma((2, 3, 2)),
            dma((2, 3, 2)),
            dma((2, 3, 2)),
            dma((8, 2)),
            dma((8, 2)),
        ],
        compiler_params=pltpu.CompilerParams(
            collective_id=1, has_side_effects=True, vmem_limit_bytes=48 * 2**20
        ),
        cost_estimate=pl.CostEstimate(
            flops=3_600_000_000, bytes_accessed=8_000_000, transcendentals=131072
        ),
        name="experts",
    )(route, weight, block_list, block_count, tokens, gate_up, down, delta)


def on_device(
    tokens,
    route,
    route_weight,
    gate_up,
    down_weight,
    adam_first,
    adam_second,
    gradient,
    block_list,
    block_count,
):
    lists = block_list[:, 0, :].T
    first_new, second_new, delta = adam(lists, adam_first, adam_second, gradient)
    mixed = expert_layer(
        route.transpose(0, 2, 1),
        route_weight.transpose(0, 2, 1),
        lists,
        block_count.T,
        tokens,
        gate_up[0],
        down_weight[0],
        delta,
    )
    return mixed, first_new, second_new


def solution(mesh):
    return jax.shard_map(
        on_device,
        mesh=mesh,
        in_specs=(
            P(None, "expert", None),
            P(None, "expert", None),
            P(None, "expert", None),
            P("expert", None, None, ("fsdp", "tensor")),
            P("expert", ("fsdp", "tensor"), None),
            P(None, ("fsdp", "tensor"), "expert"),
            P(None, ("fsdp", "tensor"), "expert"),
            P(None, ("fsdp", "tensor"), "expert"),
            P(None, ("fsdp", "tensor"), None),
            P(None, ("fsdp", "tensor")),
        ),
        out_specs=(
            P(None, "expert", ("fsdp", "tensor")),
            P(None, ("fsdp", "tensor"), "expert"),
            P(None, ("fsdp", "tensor"), "expert"),
        ),
        check_vma=False,
    )
```

```python
import functools

import jax
import jax.numpy as jnp
from jax import lax
from jax.experimental import pallas as pl
from jax.experimental.pallas import tpu as pltpu
from jax.sharding import PartitionSpec as P

F32 = jnp.float32
BF16 = jnp.bfloat16
MESH_ID = pl.DeviceIdType.MESH

E = 8
BLOCK_ROWS = 8
MAXCH = 4
CAP = 32
TOK = 64
D = 4096
HS = 256
SLOTS = E * CAP
QUART = 512
LANE = 128
KDOWN = 2 * HS + 128
NEAR = (0, 1, 7, 2, 6, 3, 5, 4)
HALF = 128
QROWS = 64
LOW = 3
VMEM_BYTES = 60 * 2**20

BETA_ONE = 0.9
BETA_TWO = 0.95
LEARN_RATE = 0.03
ADAM_EPS = 1e-08
FIRST_FIX = 1.0 - 0.9**10
SECOND_FIX = 1.0 - 0.95**10


def moments_kernel(first_part, m_in, v_in, g_in, *refs):
    m_out, v_out, one, two, grad, sems = refs[-6:]

    def loads(e):
        return [
            pltpu.make_async_copy(src.at[e], dst.at[e], sems.at[n, e])
            for n, (src, dst) in enumerate(((m_in, one), (v_in, two), (g_in, grad)))
        ]

    def stores(e):
        return [
            pltpu.make_async_copy(src.at[e], dst.at[e], sems.at[n + 3, e])
            for n, (src, dst) in enumerate(((one, m_out), (two, v_out)))
        ]

    low = lax.axis_index("expert") < LOW

    @pl.when(low if first_part else jnp.logical_not(low))
    def _():
        for e in range(E):
            for cp in loads(e):
                cp.start()
        for e in range(E):
            for cp in loads(e):
                cp.wait()
            wide = grad[e].astype(F32)
            one[e] = BETA_ONE * one[e] + (1.0 - BETA_ONE) * wide
            two[e] = BETA_TWO * two[e] + (1.0 - BETA_TWO) * wide * wide
            for cp in stores(e):
                cp.start()
        for e in range(E):
            for cp in stores(e):
                cp.wait()


def moments(first_part, *arrays):
    hbm = pl.BlockSpec(memory_space=pltpu.HBM)
    like = arrays[0]
    shape = jax.ShapeDtypeStruct(like.shape, F32)
    return pl.pallas_call(
        functools.partial(moments_kernel, first_part),
        in_specs=[hbm] * len(arrays),
        out_specs=[hbm] * 2,
        out_shape=[shape, shape],
        scratch_shapes=[
            pltpu.VMEM(like.shape, F32),
            pltpu.VMEM(like.shape, F32),
            pltpu.VMEM(like.shape, BF16),
            pltpu.SemaphoreType.DMA((5, E)),
        ],
        input_output_aliases={} if first_part else {3: 0, 4: 1},
        compiler_params=pltpu.CompilerParams(vmem_limit_bytes=VMEM_BYTES),
        name="moments_first" if first_part else "moments_last",
    )(*arrays)


def kernel(
    tokens,
    route_in,
    weight_in,
    gate_up,
    down,
    moment_one,
    moment_two,
    gradient,
    list_in,
    count_in,
    mixed,
    route_ref,
    weight_ref,
    list_ref,
    count_ref,
    one,
    two,
    grad,
    delta,
    tok,
    zsend,
    xbuf,
    gu,
    dn,
    acc,
    hid,
    mix,
    tgt,
    picks,
    far,
    via,
    near,
    held,
    came,
    own,
    r2send,
    r2recv,
    r2own,
    r3buf,
    back,
    load_sem,
    gu_sem,
    adam_sem,
    sib_send,
    sib_recv,
    z_send,
    z_recv,
    p_send,
    p_recv,
    f_send,
    f_recv,
    y_send,
    y_recv,
    d_send,
    d_recv,
    m_send,
    m_recv,
    far_s,
    far_r,
    early_s,
    early_r,
    late_s,
    late_r,
    r2s,
    r2r,
    r3s,
    r3r,
):
    x = lax.axis_index("fsdp")
    z = lax.axis_index("expert")
    t = lax.axis_index("tensor")
    y = t // 2
    c = lax.rem(t, 2)

    def at(i, j, k, core):
        return (lax.rem(x + i, 4), lax.rem(z + k, 8), lax.rem(y + j, 4) * 2 + core)

    def along(h, i):
        return at(i * (1 - h), i * h, 0, c)

    def remote(src, dst, ssem, rsem, where):
        return pltpu.make_async_remote_copy(
            src_ref=src,
            dst_ref=dst,
            send_sem=ssem,
            recv_sem=rsem,
            device_id=where,
            device_id_type=MESH_ID,
        )

    barrier = pltpu.get_barrier_semaphore()
    sibling = at(0, 0, 0, 1 - c)
    for i in range(1, 4):
        for h in range(2):
            pl.semaphore_signal(barrier, inc=1, device_id=along(h, i), device_id_type=MESH_ID)
    for k in range(8):
        pl.semaphore_signal(
            barrier, inc=1, device_id=at(0, 0, k, 1 - c), device_id_type=MESH_ID
        )
        if k:
            pl.semaphore_signal(
                barrier, inc=1, device_id=at(0, 0, k, c), device_id_type=MESH_ID
            )

    def small(src, dst, n):
        return pltpu.make_async_copy(src, dst, load_sem.at[n])

    route_load = small(route_in, route_ref, 4)
    columns = pl.ds(pl.multiple_of((4 * x + y) * 2 * LANE, 2 * LANE), 2 * LANE)
    tok_load = small(tokens.at[c, :, columns], tok, 0)
    small_loads = [
        small(list_in, list_ref, 6),
        small(count_in, count_ref, 7),
        small(weight_in, weight_ref, 8),
    ]
    adam_loads = [
        pltpu.make_async_copy(src, dst, adam_sem.at[n])
        for n, (src, dst) in enumerate(((moment_one, one), (moment_two, two), (gradient, grad)))
    ]
    down_load = small(down, dn.at[pl.ds(0, HS)], 2)
    for cp in [route_load, tok_load] + small_loads + adam_loads:
        cp.start()

    def gu_load(q):
        rows = pl.ds(pl.multiple_of(q * QUART, QUART), QUART)
        return pltpu.make_async_copy(
            gate_up.at[:, rows, :], gu.at[0, :, rows, :], gu_sem.at[q]
        )

    lower = (
        lax.broadcasted_iota(jnp.int32, (TOK, TOK), 0)
        < lax.broadcasted_iota(jnp.int32, (TOK, TOK), 1)
    ).astype(BF16)
    expert_ids = lax.broadcasted_iota(jnp.int32, (E, TOK), 0)
    slot_ids = lax.broadcasted_iota(jnp.int32, (CAP, TOK), 0).astype(F32)

    def slots_of(step):
        named = route_ref[step]
        hits = [named[k : k + 1, :] == expert_ids for k in range(2)]
        any_hit = jnp.where(hits[0] | hits[1], 1.0, 0.0)
        place = jnp.dot(any_hit.astype(BF16), lower, preferred_element_type=F32)
        place = jnp.where(any_hit > 0.5, place, -1.0)
        return hits, [slot_ids == place[e : e + 1, :] for e in range(E)]

    route_load.wait()
    _, chosen = slots_of(c)
    selector = jnp.concatenate([jnp.where(m, 1.0, 0.0) for m in chosen], axis=0).astype(BF16)
    tok_load.wait()
    picked = jnp.dot(selector, tok[...], preferred_element_type=F32).astype(BF16)
    for h in range(2):
        zsend[h] = picked[:, h * LANE : (h + 1) * LANE]
    own_rows = pl.ds(pl.multiple_of(z * CAP, CAP), CAP)
    for h in range(2):
        xbuf[h, 0, 0, pl.ds(0, CAP), :] = zsend[h, own_rows, :]

    pl.semaphore_wait(barrier, 21)

    def z_copy(n):
        rows = pl.ds(pl.multiple_of(lax.rem(z + NEAR[n], 8) * CAP, CAP), CAP)
        return remote(
            zsend.at[:, rows, :],
            xbuf.at[:, 0, 0, pl.ds(n * CAP, CAP), :],
            z_send.at[n],
            z_recv.at[n],
            at(0, 0, NEAR[n], c),
        )

    for n in range(1, 8):
        z_copy(n).start()

    def first_copy(h, i, g):
        rows = pl.ds(g * HALF, HALF)
        return remote(
            xbuf.at[h, 0, 0, rows, :],
            xbuf.at[h, 0, i, rows, :],
            p_send.at[h, i, g],
            p_recv.at[h, i, g],
            along(h, i),
        )

    def second_copy(h, w, i, g):
        rows = pl.ds(g * HALF, HALF)
        return remote(
            xbuf.at[h, 0, i, rows, :],
            xbuf.at[h, 1 + 2 * w, i, rows, :],
            f_send.at[h, w, i, g],
            f_recv.at[h, w, i, g],
            along(1 - h, 1 + 2 * w),
        )

    def relay(h, w, i, g):
        rows = pl.ds(g * HALF + w * QROWS, QROWS)
        return remote(
            xbuf.at[h, 1 + 2 * w, i, rows, :],
            xbuf.at[h, 2, i, rows, :],
            y_send.at[h, w, i, g],
            y_recv.at[h, w, i, g],
            along(1 - h, 1 + 2 * w),
        )

    def start_group(g):
        for n in range(4 * g, 4 * g + 4):
            if n:
                z_copy(n).wait_recv()
        for h in range(2):
            for w in range(2):
                first_copy(h, 1 + 2 * w, g).start()
                second_copy(h, w, 0, g).start()
            first_copy(h, 2, g).start()

    def spread(g):
        for i in (1, 3, 2):
            for h in range(2):
                first_copy(h, i, g).wait_recv()
                for w in range(2):
                    second_copy(h, w, i, g).start()

    def pass_on(i, g):
        for h in range(2):
            for w in range(2):
                second_copy(h, w, i, g).wait_recv()
                relay(h, w, i, g).start()

    def gu_swap(q):
        rows = pl.ds(pl.multiple_of(q * QUART, QUART), QUART)
        return remote(
            gate_up.at[:, rows, :],
            gu.at[1, :, rows, :],
            sib_send.at[q],
            sib_recv.at[q],
            sibling,
        )

    @pl.loop(0, 8)
    def _(q):
        gu_load(q).start()
        gu_swap(q).start()

    down_swap = remote(
        down, dn.at[pl.ds(HS, HS)], m_send.at[0], m_recv.at[0], sibling
    )
    down_swap.start()
    down_load.start()

    for cp in small_loads:
        cp.wait()
    here = lax.broadcasted_iota(jnp.int32, (MAXCH, E), 1) == z
    blocks = jnp.sum(jnp.where(here, list_ref[...], 0), axis=1, keepdims=True)
    count = jnp.sum(jnp.where(here[0:1], count_ref[...], 0), axis=1, keepdims=True)
    lane = lax.broadcasted_iota(jnp.int32, (8, LANE), 1)

    def targets(first_lane, first_unit):
        units = jnp.full((8, LANE), -1, jnp.int32)
        for j in range(MAXCH):
            start = first_lane + BLOCK_ROWS * j
            live = (lane >= start) & (lane < start + BLOCK_ROWS) & (count > j)
            unit = first_unit + 4 * (BLOCK_ROWS * blocks[j : j + 1, :] + lane - start)
            units = jnp.where(live, unit, units)
        return units.astype(F32)

    tgt[0] = targets(0, 0)
    tgt[1] = targets(CAP, HS)
    target_swap = remote(tgt.at[1], tgt.at[2], m_send.at[1], m_recv.at[1], sibling)
    target_swap.start()
    dn[pl.ds(2 * HS + 2 * CAP, 2 * CAP), :] = jnp.zeros((2 * CAP, D), BF16)

    row_ids = lax.broadcasted_iota(jnp.int32, (BLOCK_ROWS, 2 * CAP), 0)
    unit_ids = lax.broadcasted_iota(jnp.int32, (BLOCK_ROWS, 2 * CAP), 1)
    expert_lane = lax.broadcasted_iota(jnp.int32, (MAXCH, E), 1)

    def adam(e):
        wide = grad[e].astype(F32)
        top = BETA_ONE * one[e] + (1.0 - BETA_ONE) * wide
        bottom = BETA_TWO * two[e] + (1.0 - BETA_TWO) * wide * wide
        steps = -(LEARN_RATE * (top / FIRST_FIX) / (jnp.sqrt(bottom / SECOND_FIX) + ADAM_EPS))
        numbers = jnp.sum(
            jnp.where(expert_lane == e, list_ref[...], 0), axis=1, keepdims=True
        )
        taken = [
            jnp.where(unit_ids == BLOCK_ROWS * numbers[j : j + 1, :] + row_ids, 1.0, 0.0)
            for j in range(MAXCH)
        ]
        delta[e] = jnp.dot(
            jnp.concatenate(taken, axis=0).astype(BF16),
            steps.astype(BF16),
            preferred_element_type=F32,
        ).astype(BF16)

    for cp in adam_loads:
        cp.wait()

    @pl.loop(0, 4)
    def _(e):
        adam(e)

    start_group(0)

    @pl.loop(4, 8)
    def _(e):
        adam(e)

    start_group(1)

    delta_cols = pl.ds(pl.multiple_of(z * QUART, QUART), QUART)

    def d_copy(k):
        e = lax.rem(z + k, 8)
        return remote(
            delta.at[e],
            dn.at[pl.ds(2 * HS, CAP), delta_cols],
            d_send.at[k],
            d_recv.at[k],
            at(0, 0, k, c),
        )

    @pl.loop(1, 8)
    def _(k):
        d_copy(k).start()

    dn[pl.ds(2 * HS, CAP), delta_cols] = delta[z]
    spread(0)
    pass_on(0, 0)
    spread(1)
    pass_on(0, 1)

    def project(h, j, first):
        block = jnp.concatenate([xbuf[h, j, i] for i in range(4)], axis=1)
        for s in range(2):
            for g in range(2):
                parts = []
                for i in range(4):
                    a, b = i + h * (j - i), j + h * (i - j)
                    chip = 4 * lax.rem(x - a + 4, 4) + lax.rem(y - b + 4, 4)
                    rows = pl.ds(pl.multiple_of(chip * 2 * LANE + h * LANE, LANE), LANE)
                    parts.append(gu[s, g, rows, :])
                term = jnp.dot(
                    block, jnp.concatenate(parts, axis=0), preferred_element_type=F32
                )
                if first:
                    acc[2 * s + g] = term
                else:
                    acc[2 * s + g] += term

    @pl.loop(0, 8)
    def _(q):
        gu_load(q).wait()
        gu_swap(q).wait_recv()

    for g in range(2):
        for i in (1, 3, 2):
            pass_on(i, g)
    project(0, 0, True)
    project(1, 0, False)

    for k in range(1, 8):
        d_copy(k).wait_recv()
    delta_swap = remote(
        dn.at[pl.ds(2 * HS, CAP)],
        dn.at[pl.ds(2 * HS + CAP, CAP)],
        m_send.at[2],
        m_recv.at[2],
        sibling,
    )
    delta_swap.start()

    target_swap.wait_recv()
    unit = jnp.where(lane < CAP, tgt[0], tgt[2])[0:1, :]
    picks[...] = (
        lax.broadcasted_iota(jnp.int32, (2 * HS, LANE), 0).astype(F32) == unit
    ).astype(BF16)

    for step in range(2):
        hits, chosen = slots_of(step)
        w = weight_ref[step]
        by_expert = jnp.where(hits[0], w[0:1, :], 0.0) + jnp.where(hits[1], w[1:2, :], 0.0)
        full = jnp.concatenate(
            [jnp.where(chosen[e], by_expert[e : e + 1, :], 0.0) for e in range(E)], axis=0
        )
        full = full.T
        high = full.astype(BF16)
        mix[step, pl.ds(0, TOK), :] = high
        mix[step, pl.ds(TOK, TOK), :] = (full - high.astype(F32)).astype(BF16)

    @pl.loop(0, 4)
    def _(q):
        project(lax.rem(q, 2), 1 + 2 * (q // 2), False)

    for h in range(2):
        for i in range(4):
            for g in range(2):
                for w in range(2):
                    relay(h, w, i, g).wait_recv()
        project(h, 2, False)

    for s in range(2):
        gate = acc[2 * s]
        hid[:, pl.ds(s * HS, HS)] = (jax.nn.silu(gate) * acc[2 * s + 1]).astype(BF16)
    hid[:, pl.ds(2 * HS, LANE)] = jnp.dot(
        hid[:, pl.ds(0, 2 * HS)], picks[...], preferred_element_type=F32
    ).astype(BF16)

    down_load.wait()
    down_swap.wait_recv()
    delta_swap.wait_recv()

    def down_term(h, i):
        cols = []
        for j in range(4):
            a, b = i + h * (j - i), j + h * (i - j)
            block = 8 * lax.rem(x + a, 4) + 2 * lax.rem(y + b, 4) + h
            cols.append(dn[:, pl.ds(pl.multiple_of(block * LANE, LANE), LANE)])
        return jnp.dot(hid[...], jnp.concatenate(cols, axis=1), preferred_element_type=F32)

    def far_copy(h, w, b):
        return remote(
            far.at[h, pl.ds(w * HALF + (1 - b) * QROWS, QROWS), :],
            via.at[h, w, pl.ds((1 - b) * QROWS, QROWS), :],
            far_s.at[h, w, b],
            far_r.at[h, w, b],
            along(h, 1 + 2 * w),
        )

    def early_copy(h, w):
        rows = pl.ds((1 - w) * HALF, HALF)
        return remote(
            near.at[h, w, rows, :],
            came.at[h, w, rows, :],
            early_s.at[h, w],
            early_r.at[h, w],
            along(h, 1 + 2 * w),
        )

    def late_copy(h, w, b):
        rows = pl.ds(w * HALF + (1 - b) * QROWS, QROWS)
        return remote(
            near.at[h, w, rows, :],
            came.at[h, w, rows, :],
            late_s.at[h, w, b],
            late_r.at[h, w, b],
            along(h, 1 + 2 * w),
        )

    @pl.loop(0, 2)
    def _(h):
        far[h] = down_term(h, 2).astype(BF16)
        for b in range(2):
            for w in range(2):
                far_copy(h, w, b).start()

    for w in range(2):

        @pl.loop(0, 2)
        def _(h):
            term = down_term(h, 1 + 2 * w)
            direct = (1 - w) * HALF
            near[h, w, pl.ds(direct, HALF), :] = term[direct : direct + HALF].astype(BF16)
            early_copy(h, w).start()
            held[h, w] = term[w * HALF : (w + 1) * HALF]

    @pl.loop(0, 2)
    def _(h):
        own[h] = down_term(h, 0)

    for b in range(2):
        rows = pl.ds((1 - b) * QROWS, QROWS)
        for h in range(2):
            for w in range(2):
                far_copy(h, w, b).wait_recv()
                near[h, w, pl.ds(w * HALF + (1 - b) * QROWS, QROWS), :] = (
                    held[h, w, rows, :] + via[h, w, rows, :].astype(F32)
                ).astype(BF16)
                late_copy(h, w, b).start()

    def r2_copy(h, j, b):
        return remote(
            r2send.at[h, j - 1, b],
            r2recv.at[h, j - 1, b],
            r2s.at[h, j - 1, b],
            r2r.at[h, j - 1, b],
            along(1 - h, j),
        )

    for b in range(2):
        for h in range(2):
            for w in range(2):
                if b == 0:
                    early_copy(h, w).wait_recv()
                late_copy(h, w, b).wait_recv()
            for m in range(2):
                rows = pl.ds(m * HALF + (1 - b) * QROWS, QROWS)
                put = pl.ds(m * QROWS, QROWS)
                for j in (2, 1, 3, 0):
                    cols = pl.ds(j * LANE, LANE)
                    total = (
                        own[h, rows, cols]
                        + came[h, 0, rows, cols].astype(F32)
                        + came[h, 1, rows, cols].astype(F32)
                    )
                    if j:
                        r2send[h, j - 1, b, put, :] = total.astype(BF16)
                    else:
                        r2own[h, b, put, :] = total
            for j in (2, 1, 3):
                r2_copy(h, j, b).start()

    def r3_rows(n):
        return 1 - (n // 2) % 2, pl.ds((n % 2) * CAP + (n // 4) * QROWS, CAP)

    def r3_copy(h, n):
        b, rows = r3_rows(n)
        return remote(
            r3buf.at[h, b, rows, :],
            back.at[c, own_rows, :],
            r3s.at[n, h],
            r3r.at[n, c],
            at(0, 0, 8 - NEAR[n], h),
        )

    def r3_wait(step, n):
        rows = pl.ds(pl.multiple_of(lax.rem(z + NEAR[n], 8) * CAP, CAP), CAP)
        remote(
            back.at[step, rows, :],
            back.at[step, rows, :],
            r3s.at[n, step],
            r3r.at[n, step],
            at(0, 0, NEAR[n], step),
        ).wait_recv()

    for b in range(2):
        for h in range(2):
            for j in (1, 3, 2):
                r2_copy(h, j, b).wait_recv()
            total = r2own[h, b]
            for j in range(3):
                total += r2recv[h, j, b].astype(F32)
            r3buf[h, b] = total.astype(BF16)
            for n in (7, 6, 3, 2) if b == 0 else (5, 4, 1):
                r3_copy(h, n).start()
    r3_copy(1 - c, 0).start()
    b, rows = r3_rows(0)
    back[c, own_rows, :] = r3buf[c, b, rows, :]
    r3_wait(1 - c, 0)
    for step in range(2):
        for n in range(1, 8):
            r3_wait(step, n)
        both = jnp.dot(mix[step], back[step], preferred_element_type=F32)
        mixed[step] = (both[:TOK] + both[TOK:]).astype(BF16)

    r3_copy(1 - c, 0).wait_send()
    for n in range(1, 8):
        z_copy(n).wait_send()
        for h in range(2):
            r3_copy(h, n).wait_send()
    for h in range(2):
        for g in range(2):
            for i in range(4):
                if i:
                    first_copy(h, i, g).wait_send()
                for w in range(2):
                    second_copy(h, w, i, g).wait_send()
                    relay(h, w, i, g).wait_send()
        for w in range(2):
            early_copy(h, w).wait_send()
            for b in range(2):
                far_copy(h, w, b).wait_send()
                late_copy(h, w, b).wait_send()
        for j in range(1, 4):
            for b in range(2):
                r2_copy(h, j, b).wait_send()

    @pl.loop(0, 8)
    def _(q):
        gu_swap(q).wait_send()

    for k in range(1, 8):
        d_copy(k).wait_send()
    for cp in (down_swap, target_swap, delta_swap):
        cp.wait_send()


def experts(*args):
    hbm = pl.BlockSpec(memory_space=pltpu.HBM)
    dma = pltpu.SemaphoreType.DMA
    rows, cols = args[5].shape[1:]
    return pl.pallas_call(
        kernel,
        in_specs=[hbm] * 10,
        out_specs=pl.BlockSpec(memory_space=pltpu.VMEM),
        out_shape=pltpu.VMEM((2, TOK, LANE), BF16),
        scratch_shapes=[
            pltpu.VMEM((2, 2, TOK), jnp.int32),
            pltpu.VMEM((2, 2, TOK), F32),
            pltpu.VMEM((MAXCH, E), jnp.int32),
            pltpu.VMEM((1, E), jnp.int32),
            pltpu.VMEM((E, rows, cols), F32),
            pltpu.VMEM((E, rows, cols), F32),
            pltpu.VMEM((E, rows, cols), BF16),
            pltpu.VMEM((E, CAP, cols), BF16),
            pltpu.VMEM((TOK, 2 * LANE), BF16),
            pltpu.VMEM((2, SLOTS, LANE), BF16),
            pltpu.VMEM((2, 4, 4, SLOTS, LANE), BF16),
            pltpu.VMEM((2, 2, D, HS), BF16),
            pltpu.VMEM((KDOWN, D), BF16),
            pltpu.VMEM((4, SLOTS, HS), F32),
            pltpu.VMEM((SLOTS, KDOWN), BF16),
            pltpu.VMEM((2, 2 * TOK, SLOTS), BF16),
            pltpu.VMEM((3, 8, LANE), F32),
            pltpu.VMEM((2 * HS, LANE), BF16),
            pltpu.VMEM((2, SLOTS, QUART), BF16),
            pltpu.VMEM((2, 2, HALF, QUART), BF16),
            pltpu.VMEM((2, 2, SLOTS, QUART), BF16),
            pltpu.VMEM((2, 2, HALF, QUART), F32),
            pltpu.VMEM((2, 2, SLOTS, QUART), BF16),
            pltpu.VMEM((2, SLOTS, QUART), F32),
            pltpu.VMEM((2, 3, 2, HALF, LANE), BF16),
            pltpu.VMEM((2, 3, 2, HALF, LANE), BF16),
            pltpu.VMEM((2, 2, HALF, LANE), F32),
            pltpu.VMEM((2, 2, HALF, LANE), BF16),
            pltpu.VMEM((2, SLOTS, LANE), BF16),
            dma((9,)),
            dma((8,)),
            dma((3,)),
            dma((8,)),
            dma((8,)),
            dma((8,)),
            dma((8,)),
            dma((2, 4, 2)),
            dma((2, 4, 2)),
            dma((2, 2, 4, 2)),
            dma((2, 2, 4, 2)),
            dma((2, 2, 4, 2)),
            dma((2, 2, 4, 2)),
            dma((8,)),
            dma((8,)),
            dma((3,)),
            dma((3,)),
            dma((2, 2, 2)),
            dma((2, 2, 2)),
            dma((2, 2)),
            dma((2, 2)),
            dma((2, 2, 2)),
            dma((2, 2, 2)),
            dma((2, 3, 2)),
            dma((2, 3, 2)),
            dma((8, 2)),
            dma((8, 2)),
        ],
        compiler_params=pltpu.CompilerParams(
            collective_id=1, has_side_effects=True, vmem_limit_bytes=VMEM_BYTES
        ),
        cost_estimate=pl.CostEstimate(
            flops=3_600_000_000, bytes_accessed=12_000_000, transcendentals=400_000
        ),
        name="experts",
    )(*args)


def on_device(
    tokens,
    route,
    route_weight,
    gate_up,
    down_weight,
    adam_first,
    adam_second,
    gradient,
    block_list,
    block_count,
):
    inputs = (adam_first, adam_second, gradient)
    made = moments(True, *inputs)
    *made, tokens = lax.optimization_barrier((*made, tokens))
    mixed = experts(
        tokens,
        route.transpose(0, 2, 1),
        route_weight.transpose(0, 2, 1),
        gate_up[0],
        down_weight[0],
        adam_first,
        adam_second,
        gradient,
        block_list[:, 0, :].T,
        block_count.T,
    )
    *made, mixed = lax.optimization_barrier((*made, mixed))
    return mixed, *moments(False, *inputs, *made)


def solution(mesh):
    return jax.shard_map(
        on_device,
        mesh=mesh,
        in_specs=(
            P(None, "expert", None),
            P(None, "expert", None),
            P(None, "expert", None),
            P("expert", None, None, ("fsdp", "tensor")),
            P("expert", ("fsdp", "tensor"), None),
            P(None, ("fsdp", "tensor"), "expert"),
            P(None, ("fsdp", "tensor"), "expert"),
            P(None, ("fsdp", "tensor"), "expert"),
            P(None, ("fsdp", "tensor"), None),
            P(None, ("fsdp", "tensor")),
        ),
        out_specs=(
            P(None, "expert", ("fsdp", "tensor")),
            P(None, ("fsdp", "tensor"), "expert"),
            P(None, ("fsdp", "tensor"), "expert"),
        ),
        check_vma=False,
    )
```

```python
import functools

import jax
import jax.numpy as jnp
from jax import lax
from jax.experimental import pallas as pl
from jax.experimental.pallas import tpu as pltpu
from jax.sharding import PartitionSpec as P

F32 = jnp.float32
BF16 = jnp.bfloat16
MESH_ID = pl.DeviceIdType.MESH

E = 8
BLOCK_ROWS = 8
MAXCH = 4
CAP = 32
TOK = 64
D = 4096
HS = 256
SLOTS = E * CAP
QUART = 512
LANE = 128
KDOWN = 2 * HS + 128
NEAR = (0, 1, 7, 2, 6, 3, 5, 4)
WIDE = 1
GROUPS = ((1, 5), (5, 8))
HALF = 128
QROWS = 64
LOW = 3
VMEM_BYTES = 60 * 2**20

BETA_ONE = 0.9
BETA_TWO = 0.95
LEARN_RATE = 0.03
ADAM_EPS = 1e-08
FIRST_FIX = 1.0 - 0.9**10
SECOND_FIX = 1.0 - 0.95**10


def moments_kernel(first_part, m_in, v_in, g_in, *refs):
    m_out, v_out, one, two, grad, sems = refs[-6:]

    def loads(e):
        return [
            pltpu.make_async_copy(src.at[e], dst.at[e], sems.at[n, e])
            for n, (src, dst) in enumerate(((m_in, one), (v_in, two), (g_in, grad)))
        ]

    def stores(e):
        return [
            pltpu.make_async_copy(src.at[e], dst.at[e], sems.at[n + 3, e])
            for n, (src, dst) in enumerate(((one, m_out), (two, v_out)))
        ]

    low = lax.axis_index("expert") < LOW

    @pl.when(low if first_part else jnp.logical_not(low))
    def _():
        for e in range(E):
            for cp in loads(e):
                cp.start()
        for e in range(E):
            for cp in loads(e):
                cp.wait()
            wide = grad[e].astype(F32)
            one[e] = BETA_ONE * one[e] + (1.0 - BETA_ONE) * wide
            two[e] = BETA_TWO * two[e] + (1.0 - BETA_TWO) * wide * wide
            for cp in stores(e):
                cp.start()
        for e in range(E):
            for cp in stores(e):
                cp.wait()


def moments(first_part, *arrays):
    hbm = pl.BlockSpec(memory_space=pltpu.HBM)
    like = arrays[0]
    shape = jax.ShapeDtypeStruct(like.shape, F32)
    return pl.pallas_call(
        functools.partial(moments_kernel, first_part),
        in_specs=[hbm] * len(arrays),
        out_specs=[hbm] * 2,
        out_shape=[shape, shape],
        scratch_shapes=[
            pltpu.VMEM(like.shape, F32),
            pltpu.VMEM(like.shape, F32),
            pltpu.VMEM(like.shape, BF16),
            pltpu.SemaphoreType.DMA((5, E)),
        ],
        input_output_aliases={} if first_part else {3: 0, 4: 1},
        compiler_params=pltpu.CompilerParams(vmem_limit_bytes=VMEM_BYTES),
        name="moments_first" if first_part else "moments_last",
    )(*arrays)


def kernel(
    tokens,
    route_in,
    weight_in,
    gate_up,
    down,
    moment_one,
    moment_two,
    gradient,
    list_in,
    count_in,
    mixed,
    route_ref,
    weight_ref,
    list_ref,
    count_ref,
    one,
    two,
    grad,
    delta,
    tok,
    full,
    selector,
    wide,
    zsend,
    xbuf,
    gu,
    dn,
    acc,
    hid,
    mix,
    tgt,
    picks,
    far,
    via,
    near,
    held,
    came,
    own,
    r2send,
    r2recv,
    r2own,
    r3buf,
    back,
    load_sem,
    gu_sem,
    adam_sem,
    sib_send,
    sib_recv,
    z_send,
    z_recv,
    w_send,
    w_recv,
    p_send,
    p_recv,
    f_send,
    f_recv,
    y_send,
    y_recv,
    d_send,
    d_recv,
    m_send,
    m_recv,
    far_s,
    far_r,
    early_s,
    early_r,
    late_s,
    late_r,
    r2s,
    r2r,
    r3s,
    r3r,
):
    x = lax.axis_index("fsdp")
    z = lax.axis_index("expert")
    t = lax.axis_index("tensor")
    y = t // 2
    c = lax.rem(t, 2)

    def at(i, j, k, core):
        return (lax.rem(x + i, 4), lax.rem(z + k, 8), lax.rem(y + j, 4) * 2 + core)

    def along(h, i):
        return at(i * (1 - h), i * h, 0, c)

    def remote(src, dst, ssem, rsem, where):
        return pltpu.make_async_remote_copy(
            src_ref=src,
            dst_ref=dst,
            send_sem=ssem,
            recv_sem=rsem,
            device_id=where,
            device_id_type=MESH_ID,
        )

    barrier = pltpu.get_barrier_semaphore()
    sibling = at(0, 0, 0, 1 - c)
    for i in range(1, 4):
        for h in range(2):
            pl.semaphore_signal(barrier, inc=1, device_id=along(h, i), device_id_type=MESH_ID)
    for k in range(8):
        pl.semaphore_signal(
            barrier, inc=1, device_id=at(0, 0, k, 1 - c), device_id_type=MESH_ID
        )
        if k:
            pl.semaphore_signal(
                barrier, inc=1, device_id=at(0, 0, k, c), device_id_type=MESH_ID
            )

    def small(src, dst, n):
        return pltpu.make_async_copy(src, dst, load_sem.at[n])

    route_load = small(route_in, route_ref, 4)
    columns = pl.ds(pl.multiple_of((4 * x + y) * 2 * LANE, 2 * LANE), 2 * LANE)
    tok_load = small(tokens.at[c, :, columns], tok, 0)
    full_load = small(tokens.at[c], full, 1)
    small_loads = [
        small(list_in, list_ref, 6),
        small(count_in, count_ref, 7),
        small(weight_in, weight_ref, 8),
    ]
    adam_loads = [
        pltpu.make_async_copy(src, dst, adam_sem.at[n])
        for n, (src, dst) in enumerate(((moment_one, one), (moment_two, two), (gradient, grad)))
    ]
    down_load = small(down, dn.at[pl.ds(0, HS)], 2)
    for cp in [route_load, tok_load, full_load] + small_loads + adam_loads:
        cp.start()

    def gu_load(q):
        rows = pl.ds(pl.multiple_of(q * QUART, QUART), QUART)
        return pltpu.make_async_copy(
            gate_up.at[:, rows, :], gu.at[0, :, rows, :], gu_sem.at[q]
        )

    lower = (
        lax.broadcasted_iota(jnp.int32, (TOK, TOK), 0)
        < lax.broadcasted_iota(jnp.int32, (TOK, TOK), 1)
    ).astype(BF16)
    expert_ids = lax.broadcasted_iota(jnp.int32, (E, TOK), 0)
    slot_ids = lax.broadcasted_iota(jnp.int32, (CAP, TOK), 0).astype(F32)

    def slots_of(step):
        named = route_ref[step]
        hits = [named[k : k + 1, :] == expert_ids for k in range(2)]
        any_hit = jnp.where(hits[0] | hits[1], 1.0, 0.0)
        place = jnp.dot(any_hit.astype(BF16), lower, preferred_element_type=F32)
        place = jnp.where(any_hit > 0.5, place, -1.0)
        return hits, [slot_ids == place[e : e + 1, :] for e in range(E)]

    route_load.wait()
    _, chosen = slots_of(c)
    selector[...] = jnp.concatenate(
        [jnp.where(m, 1.0, 0.0) for m in chosen], axis=0
    ).astype(BF16)
    tok_load.wait()
    picked = jnp.dot(selector[...], tok[...], preferred_element_type=F32).astype(BF16)
    for h in range(2):
        zsend[h] = picked[:, h * LANE : (h + 1) * LANE]

    def expert_rows(n):
        return pl.ds(pl.multiple_of(lax.rem(z + NEAR[n], 8) * CAP, CAP), CAP)

    own_rows = expert_rows(0)

    pl.semaphore_wait(barrier, 21)

    def z_copy(n):
        return remote(
            zsend.at[:, expert_rows(n), :],
            xbuf.at[:, 0, 0, pl.ds(n * CAP, CAP), :],
            z_send.at[n],
            z_recv.at[n],
            at(0, 0, NEAR[n], c),
        )

    def wide_copy(n, h):
        return remote(
            wide.at[n - 1, h],
            xbuf.at[h, :, :, pl.ds(n * CAP, CAP), :],
            w_send.at[n, h],
            w_recv.at[n, h],
            at(0, 0, NEAR[n], c),
        )

    for n in range(7, WIDE - 1, -1):
        z_copy(n).start()

    def group(g):
        start, end = GROUPS[g]
        return pl.ds(start * CAP, (end - start) * CAP)

    def half_group(g, w):
        start, end = GROUPS[g]
        size = (end - start) * CAP // 2
        return pl.ds(start * CAP + w * size, size)

    def first_copy(h, i, g):
        rows = group(g)
        return remote(
            xbuf.at[h, 0, 0, rows, :],
            xbuf.at[h, 0, i, rows, :],
            p_send.at[h, i, g],
            p_recv.at[h, i, g],
            along(h, i),
        )

    def second_copy(h, w, i, g):
        rows = group(g)
        return remote(
            xbuf.at[h, 0, i, rows, :],
            xbuf.at[h, 1 + 2 * w, i, rows, :],
            f_send.at[h, w, i, g],
            f_recv.at[h, w, i, g],
            along(1 - h, 1 + 2 * w),
        )

    def relay(h, w, i, g):
        rows = half_group(g, w)
        return remote(
            xbuf.at[h, 1 + 2 * w, i, rows, :],
            xbuf.at[h, 2, i, rows, :],
            y_send.at[h, w, i, g],
            y_recv.at[h, w, i, g],
            along(1 - h, 1 + 2 * w),
        )

    def start_group(g):
        for n in range(*GROUPS[g]):
            z_copy(n).wait_recv()
        for i in (2, 1, 3):
            for h in range(2):
                first_copy(h, i, g).start()
        for h in range(2):
            for w in range(2):
                second_copy(h, w, 0, g).start()

    def spread(g):
        for i in (1, 3, 2):
            for h in range(2):
                first_copy(h, i, g).wait_recv()
                for w in range(2):
                    second_copy(h, w, i, g).start()

    def pass_on(i, g):
        for h in range(2):
            for w in range(2):
                second_copy(h, w, i, g).wait_recv()
                relay(h, w, i, g).start()

    def gu_swap(q):
        rows = pl.ds(pl.multiple_of(q * QUART, QUART), QUART)
        return remote(
            gate_up.at[:, rows, :],
            gu.at[1, :, rows, :],
            sib_send.at[q],
            sib_recv.at[q],
            sibling,
        )

    @pl.loop(0, 8)
    def _(q):
        gu_load(q).start()
        gu_swap(q).start()

    down_swap = remote(
        down, dn.at[pl.ds(HS, HS)], m_send.at[0], m_recv.at[0], sibling
    )
    down_swap.start()
    down_load.start()

    for cp in small_loads:
        cp.wait()
    here = lax.broadcasted_iota(jnp.int32, (MAXCH, E), 1) == z
    blocks = jnp.sum(jnp.where(here, list_ref[...], 0), axis=1, keepdims=True)
    count = jnp.sum(jnp.where(here[0:1], count_ref[...], 0), axis=1, keepdims=True)
    lane = lax.broadcasted_iota(jnp.int32, (8, LANE), 1)

    def targets(first_lane, first_unit):
        units = jnp.full((8, LANE), -1, jnp.int32)
        for j in range(MAXCH):
            start = first_lane + BLOCK_ROWS * j
            live = (lane >= start) & (lane < start + BLOCK_ROWS) & (count > j)
            unit = first_unit + 4 * (BLOCK_ROWS * blocks[j : j + 1, :] + lane - start)
            units = jnp.where(live, unit, units)
        return units.astype(F32)

    tgt[0] = targets(0, 0)
    tgt[1] = targets(CAP, HS)
    target_swap = remote(tgt.at[1], tgt.at[2], m_send.at[1], m_recv.at[1], sibling)
    target_swap.start()
    dn[pl.ds(2 * HS + 2 * CAP, 2 * CAP), :] = jnp.zeros((2 * CAP, D), BF16)

    row_ids = lax.broadcasted_iota(jnp.int32, (BLOCK_ROWS, 2 * CAP), 0)
    unit_ids = lax.broadcasted_iota(jnp.int32, (BLOCK_ROWS, 2 * CAP), 1)
    expert_lane = lax.broadcasted_iota(jnp.int32, (MAXCH, E), 1)

    def adam(e):
        wide = grad[e].astype(F32)
        top = BETA_ONE * one[e] + (1.0 - BETA_ONE) * wide
        bottom = BETA_TWO * two[e] + (1.0 - BETA_TWO) * wide * wide
        steps = -(LEARN_RATE * (top / FIRST_FIX) / (jnp.sqrt(bottom / SECOND_FIX) + ADAM_EPS))
        numbers = jnp.sum(
            jnp.where(expert_lane == e, list_ref[...], 0), axis=1, keepdims=True
        )
        taken = [
            jnp.where(unit_ids == BLOCK_ROWS * numbers[j : j + 1, :] + row_ids, 1.0, 0.0)
            for j in range(MAXCH)
        ]
        delta[e] = jnp.dot(
            jnp.concatenate(taken, axis=0).astype(BF16),
            steps.astype(BF16),
            preferred_element_type=F32,
        ).astype(BF16)

    for cp in adam_loads:
        cp.wait()

    @pl.loop(0, 4)
    def _(e):
        adam(e)

    start_group(0)

    @pl.loop(4, 8)
    def _(e):
        adam(e)

    delta_cols = pl.ds(pl.multiple_of(z * QUART, QUART), QUART)

    def d_copy(k):
        e = lax.rem(z + k, 8)
        return remote(
            delta.at[e],
            dn.at[pl.ds(2 * HS, CAP), delta_cols],
            d_send.at[k],
            d_recv.at[k],
            at(0, 0, k, c),
        )

    @pl.loop(1, 8)
    def _(k):
        d_copy(k).start()

    dn[pl.ds(2 * HS, CAP), delta_cols] = delta[z]
    start_group(1)

    full_load.wait()

    @pl.loop(0, 8)
    def _(q):
        h, j = q // 4, lax.rem(q, 4)
        parts = []
        for i in range(4):
            a, b = i + h * (j - i), j + h * (i - j)
            chip = 4 * lax.rem(x - a + 4, 4) + lax.rem(y - b + 4, 4)
            start = pl.multiple_of(chip * 2 * LANE + h * LANE, LANE)
            parts.append(full[:, pl.ds(start, LANE)])
        block = jnp.concatenate(parts, axis=1)
        for n in range(WIDE):
            rows = jnp.dot(
                selector[expert_rows(n), :], block, preferred_element_type=F32
            ).astype(BF16)
            for i in range(4):
                piece = rows[:, i * LANE : (i + 1) * LANE]
                if n:
                    wide[n - 1, h, j, i] = piece
                else:
                    xbuf[h, j, i, pl.ds(0, CAP), :] = piece

    for n in range(1, WIDE):
        for h in range(2):
            wide_copy(n, h).start()


    spread(0)
    pass_on(0, 0)
    spread(1)
    pass_on(0, 1)

    def project(h, j, first):
        block = jnp.concatenate([xbuf[h, j, i] for i in range(4)], axis=1)
        for s in range(2):
            for g in range(2):
                parts = []
                for i in range(4):
                    a, b = i + h * (j - i), j + h * (i - j)
                    chip = 4 * lax.rem(x - a + 4, 4) + lax.rem(y - b + 4, 4)
                    rows = pl.ds(pl.multiple_of(chip * 2 * LANE + h * LANE, LANE), LANE)
                    parts.append(gu[s, g, rows, :])
                term = jnp.dot(
                    block, jnp.concatenate(parts, axis=0), preferred_element_type=F32
                )
                if first:
                    acc[2 * s + g] = term
                else:
                    acc[2 * s + g] += term

    @pl.loop(0, 8)
    def _(q):
        gu_load(q).wait()
        gu_swap(q).wait_recv()

    for g in range(2):
        for i in (1, 3, 2):
            pass_on(i, g)
    for n in range(1, WIDE):
        for h in range(2):
            wide_copy(n, h).wait_recv()
    project(0, 0, True)
    project(1, 0, False)

    for k in range(1, 8):
        d_copy(k).wait_recv()
    delta_swap = remote(
        dn.at[pl.ds(2 * HS, CAP)],
        dn.at[pl.ds(2 * HS + CAP, CAP)],
        m_send.at[2],
        m_recv.at[2],
        sibling,
    )
    delta_swap.start()

    target_swap.wait_recv()
    unit = jnp.where(lane < CAP, tgt[0], tgt[2])[0:1, :]
    picks[...] = (
        lax.broadcasted_iota(jnp.int32, (2 * HS, LANE), 0).astype(F32) == unit
    ).astype(BF16)

    for step in range(2):
        hits, chosen = slots_of(step)
        w = weight_ref[step]
        by_expert = jnp.where(hits[0], w[0:1, :], 0.0) + jnp.where(hits[1], w[1:2, :], 0.0)
        full = jnp.concatenate(
            [jnp.where(chosen[e], by_expert[e : e + 1, :], 0.0) for e in range(E)], axis=0
        )
        full = full.T
        high = full.astype(BF16)
        mix[step, pl.ds(0, TOK), :] = high
        mix[step, pl.ds(TOK, TOK), :] = (full - high.astype(F32)).astype(BF16)

    @pl.loop(0, 4)
    def _(q):
        project(lax.rem(q, 2), 1 + 2 * (q // 2), False)

    for h in range(2):
        for i in range(4):
            for g in range(2):
                for w in range(2):
                    relay(h, w, i, g).wait_recv()
        project(h, 2, False)

    for s in range(2):
        gate = acc[2 * s]
        hid[:, pl.ds(s * HS, HS)] = (jax.nn.silu(gate) * acc[2 * s + 1]).astype(BF16)
    hid[:, pl.ds(2 * HS, LANE)] = jnp.dot(
        hid[:, pl.ds(0, 2 * HS)], picks[...], preferred_element_type=F32
    ).astype(BF16)

    down_load.wait()
    down_swap.wait_recv()
    delta_swap.wait_recv()

    def down_term(h, i):
        cols = []
        for j in range(4):
            a, b = i + h * (j - i), j + h * (i - j)
            block = 8 * lax.rem(x + a, 4) + 2 * lax.rem(y + b, 4) + h
            cols.append(dn[:, pl.ds(pl.multiple_of(block * LANE, LANE), LANE)])
        return jnp.dot(hid[...], jnp.concatenate(cols, axis=1), preferred_element_type=F32)

    def far_copy(h, w, b):
        return remote(
            far.at[h, pl.ds(w * HALF + (1 - b) * QROWS, QROWS), :],
            via.at[h, w, pl.ds((1 - b) * QROWS, QROWS), :],
            far_s.at[h, w, b],
            far_r.at[h, w, b],
            along(h, 1 + 2 * w),
        )

    def early_copy(h, w):
        rows = pl.ds((1 - w) * HALF, HALF)
        return remote(
            near.at[h, w, rows, :],
            came.at[h, w, rows, :],
            early_s.at[h, w],
            early_r.at[h, w],
            along(h, 1 + 2 * w),
        )

    def late_copy(h, w, b):
        rows = pl.ds(w * HALF + (1 - b) * QROWS, QROWS)
        return remote(
            near.at[h, w, rows, :],
            came.at[h, w, rows, :],
            late_s.at[h, w, b],
            late_r.at[h, w, b],
            along(h, 1 + 2 * w),
        )

    @pl.loop(0, 2)
    def _(h):
        far[h] = down_term(h, 2).astype(BF16)
        for b in range(2):
            for w in range(2):
                far_copy(h, w, b).start()

    for w in range(2):

        @pl.loop(0, 2)
        def _(h):
            term = down_term(h, 1 + 2 * w)
            direct = (1 - w) * HALF
            near[h, w, pl.ds(direct, HALF), :] = term[direct : direct + HALF].astype(BF16)
            early_copy(h, w).start()
            held[h, w] = term[w * HALF : (w + 1) * HALF]

    @pl.loop(0, 2)
    def _(h):
        own[h] = down_term(h, 0)

    for b in range(2):
        rows = pl.ds((1 - b) * QROWS, QROWS)
        for h in range(2):
            for w in range(2):
                far_copy(h, w, b).wait_recv()
                near[h, w, pl.ds(w * HALF + (1 - b) * QROWS, QROWS), :] = (
                    held[h, w, rows, :] + via[h, w, rows, :].astype(F32)
                ).astype(BF16)
                late_copy(h, w, b).start()

    for n in range(WIDE, 8):
        z_copy(n).wait_send()
    for n in range(1, WIDE):
        for h in range(2):
            wide_copy(n, h).wait_send()
    for h in range(2):
        for g in range(2):
            for i in range(4):
                if i:
                    first_copy(h, i, g).wait_send()
                for w in range(2):
                    second_copy(h, w, i, g).wait_send()
                    relay(h, w, i, g).wait_send()

    @pl.loop(0, 8)
    def _(q):
        gu_swap(q).wait_send()

    for k in range(1, 8):
        d_copy(k).wait_send()
    for cp in (down_swap, target_swap, delta_swap):
        cp.wait_send()

    def r2_copy(h, j, b):
        return remote(
            r2send.at[h, j - 1, b],
            r2recv.at[h, j - 1, b],
            r2s.at[h, j - 1, b],
            r2r.at[h, j - 1, b],
            along(1 - h, j),
        )

    for b in range(2):
        for h in range(2):
            for w in range(2):
                if b == 0:
                    early_copy(h, w).wait_recv()
                late_copy(h, w, b).wait_recv()
            for m in range(2):
                rows = pl.ds(m * HALF + (1 - b) * QROWS, QROWS)
                put = pl.ds(m * QROWS, QROWS)
                for j in (2, 1, 3, 0):
                    cols = pl.ds(j * LANE, LANE)
                    total = (
                        own[h, rows, cols]
                        + came[h, 0, rows, cols].astype(F32)
                        + came[h, 1, rows, cols].astype(F32)
                    )
                    if j:
                        r2send[h, j - 1, b, put, :] = total.astype(BF16)
                    else:
                        r2own[h, b, put, :] = total
            for j in (2, 1, 3):
                r2_copy(h, j, b).start()

    for h in range(2):
        for w in range(2):
            early_copy(h, w).wait_send()
            for b in range(2):
                far_copy(h, w, b).wait_send()
                late_copy(h, w, b).wait_send()

    def r3_rows(n):
        return 1 - (n // 2) % 2, pl.ds((n % 2) * CAP + (n // 4) * QROWS, CAP)

    def r3_copy(h, n):
        b, rows = r3_rows(n)
        return remote(
            r3buf.at[h, b, rows, :],
            back.at[c, own_rows, :],
            r3s.at[n, h],
            r3r.at[n, c],
            at(0, 0, 8 - NEAR[n], h),
        )

    def r3_wait(step, n):
        rows = pl.ds(pl.multiple_of(lax.rem(z + NEAR[n], 8) * CAP, CAP), CAP)
        remote(
            back.at[step, rows, :],
            back.at[step, rows, :],
            r3s.at[n, step],
            r3r.at[n, step],
            at(0, 0, NEAR[n], step),
        ).wait_recv()

    for b in range(2):
        for h in range(2):
            for j in (1, 3, 2):
                r2_copy(h, j, b).wait_recv()
            total = r2own[h, b]
            for j in range(3):
                total += r2recv[h, j, b].astype(F32)
            r3buf[h, b] = total.astype(BF16)
            for n in (7, 6, 3, 2) if b == 0 else (5, 4, 1):
                r3_copy(h, n).start()
    r3_copy(1 - c, 0).start()
    b, rows = r3_rows(0)
    back[c, own_rows, :] = r3buf[c, b, rows, :]
    for h in range(2):
        for j in range(1, 4):
            for b in range(2):
                r2_copy(h, j, b).wait_send()
    r3_wait(1 - c, 0)
    for step in range(2):
        for n in range(1, 8):
            r3_wait(step, n)
        both = jnp.dot(mix[step], back[step], preferred_element_type=F32)
        mixed[step] = (both[:TOK] + both[TOK:]).astype(BF16)

    r3_copy(1 - c, 0).wait_send()
    for n in range(1, 8):
        for h in range(2):
            r3_copy(h, n).wait_send()


def experts(*args):
    hbm = pl.BlockSpec(memory_space=pltpu.HBM)
    dma = pltpu.SemaphoreType.DMA
    rows, cols = args[5].shape[1:]
    return pl.pallas_call(
        kernel,
        in_specs=[hbm] * 10,
        out_specs=pl.BlockSpec(memory_space=pltpu.VMEM),
        out_shape=pltpu.VMEM((2, TOK, LANE), BF16),
        scratch_shapes=[
            pltpu.VMEM((2, 2, TOK), jnp.int32),
            pltpu.VMEM((2, 2, TOK), F32),
            pltpu.VMEM((MAXCH, E), jnp.int32),
            pltpu.VMEM((1, E), jnp.int32),
            pltpu.VMEM((E, rows, cols), F32),
            pltpu.VMEM((E, rows, cols), F32),
            pltpu.VMEM((E, rows, cols), BF16),
            pltpu.VMEM((E, CAP, cols), BF16),
            pltpu.VMEM((TOK, 2 * LANE), BF16),
            pltpu.VMEM((TOK, D), BF16),
            pltpu.VMEM((SLOTS, TOK), BF16),
            pltpu.VMEM((2, 2, 4, 4, CAP, LANE), BF16),
            pltpu.VMEM((2, SLOTS, LANE), BF16),
            pltpu.VMEM((2, 4, 4, SLOTS, LANE), BF16),
            pltpu.VMEM((2, 2, D, HS), BF16),
            pltpu.VMEM((KDOWN, D), BF16),
            pltpu.VMEM((4, SLOTS, HS), F32),
            pltpu.VMEM((SLOTS, KDOWN), BF16),
            pltpu.VMEM((2, 2 * TOK, SLOTS), BF16),
            pltpu.VMEM((3, 8, LANE), F32),
            pltpu.VMEM((2 * HS, LANE), BF16),
            pltpu.VMEM((2, SLOTS, QUART), BF16),
            pltpu.VMEM((2, 2, HALF, QUART), BF16),
            pltpu.VMEM((2, 2, SLOTS, QUART), BF16),
            pltpu.VMEM((2, 2, HALF, QUART), F32),
            pltpu.VMEM((2, 2, SLOTS, QUART), BF16),
            pltpu.VMEM((2, SLOTS, QUART), F32),
            pltpu.VMEM((2, 3, 2, HALF, LANE), BF16),
            pltpu.VMEM((2, 3, 2, HALF, LANE), BF16),
            pltpu.VMEM((2, 2, HALF, LANE), F32),
            pltpu.VMEM((2, 2, HALF, LANE), BF16),
            pltpu.VMEM((2, SLOTS, LANE), BF16),
            dma((9,)),
            dma((8,)),
            dma((3,)),
            dma((8,)),
            dma((8,)),
            dma((8,)),
            dma((8,)),
            dma((3, 2)),
            dma((3, 2)),
            dma((2, 4, 2)),
            dma((2, 4, 2)),
            dma((2, 2, 4, 2)),
            dma((2, 2, 4, 2)),
            dma((2, 2, 4, 2)),
            dma((2, 2, 4, 2)),
            dma((8,)),
            dma((8,)),
            dma((3,)),
            dma((3,)),
            dma((2, 2, 2)),
            dma((2, 2, 2)),
            dma((2, 2)),
            dma((2, 2)),
            dma((2, 2, 2)),
            dma((2, 2, 2)),
            dma((2, 3, 2)),
            dma((2, 3, 2)),
            dma((8, 2)),
            dma((8, 2)),
        ],
        compiler_params=pltpu.CompilerParams(
            collective_id=1, has_side_effects=True, vmem_limit_bytes=VMEM_BYTES
        ),
        cost_estimate=pl.CostEstimate(
            flops=3_600_000_000, bytes_accessed=12_000_000, transcendentals=400_000
        ),
        name="experts",
    )(*args)


def on_device(
    tokens,
    route,
    route_weight,
    gate_up,
    down_weight,
    adam_first,
    adam_second,
    gradient,
    block_list,
    block_count,
):
    inputs = (adam_first, adam_second, gradient)
    made = moments(True, *inputs)
    *made, tokens = lax.optimization_barrier((*made, tokens))
    mixed = experts(
        tokens,
        route.transpose(0, 2, 1),
        route_weight.transpose(0, 2, 1),
        gate_up[0],
        down_weight[0],
        adam_first,
        adam_second,
        gradient,
        block_list[:, 0, :].T,
        block_count.T,
    )
    *made, mixed = lax.optimization_barrier((*made, mixed))
    return mixed, *moments(False, *inputs, *made)


def solution(mesh):
    return jax.shard_map(
        on_device,
        mesh=mesh,
        in_specs=(
            P(None, "expert", None),
            P(None, "expert", None),
            P(None, "expert", None),
            P("expert", None, None, ("fsdp", "tensor")),
            P("expert", ("fsdp", "tensor"), None),
            P(None, ("fsdp", "tensor"), "expert"),
            P(None, ("fsdp", "tensor"), "expert"),
            P(None, ("fsdp", "tensor"), "expert"),
            P(None, ("fsdp", "tensor"), None),
            P(None, ("fsdp", "tensor")),
        ),
        out_specs=(
            P(None, "expert", ("fsdp", "tensor")),
            P(None, ("fsdp", "tensor"), "expert"),
            P(None, ("fsdp", "tensor"), "expert"),
        ),
        check_vma=False,
    )
```

```python
import functools

import jax
import jax.numpy as jnp
from jax import lax
from jax.experimental import pallas as pl
from jax.experimental.pallas import tpu as pltpu
from jax.sharding import PartitionSpec as P

F32 = jnp.float32
BF16 = jnp.bfloat16
MESH_ID = pl.DeviceIdType.MESH

E = 8
BLOCK_ROWS = 8
MAXCH = 4
CAP = 32
TOK = 64
D = 4096
HS = 256
SLOTS = E * CAP
QUART = 512
LANE = 128
KDOWN = 2 * HS + 128
NEAR = (0, 1, 7, 2, 6, 3, 5, 4)
WIDE = 1
GROUPS = ((1, 4), (4, 8))
HALF = 128
QROWS = 64
LOW = 3
VMEM_BYTES = 60 * 2**20

BETA_ONE = 0.9
BETA_TWO = 0.95
LEARN_RATE = 0.03
ADAM_EPS = 1e-08
FIRST_FIX = 1.0 - 0.9**10
SECOND_FIX = 1.0 - 0.95**10


def moments_kernel(first_part, m_in, v_in, g_in, *refs):
    m_out, v_out, one, two, grad, sems = refs[-6:]

    def loads(e):
        return [
            pltpu.make_async_copy(src.at[e], dst.at[e], sems.at[n, e])
            for n, (src, dst) in enumerate(((m_in, one), (v_in, two), (g_in, grad)))
        ]

    def stores(e):
        return [
            pltpu.make_async_copy(src.at[e], dst.at[e], sems.at[n + 3, e])
            for n, (src, dst) in enumerate(((one, m_out), (two, v_out)))
        ]

    low = lax.axis_index("expert") < LOW

    @pl.when(low if first_part else jnp.logical_not(low))
    def _():
        for e in range(E):
            for cp in loads(e):
                cp.start()
        for e in range(E):
            for cp in loads(e):
                cp.wait()
            wide = grad[e].astype(F32)
            one[e] = BETA_ONE * one[e] + (1.0 - BETA_ONE) * wide
            two[e] = BETA_TWO * two[e] + (1.0 - BETA_TWO) * wide * wide
            for cp in stores(e):
                cp.start()
        for e in range(E):
            for cp in stores(e):
                cp.wait()


def moments(first_part, *arrays):
    hbm = pl.BlockSpec(memory_space=pltpu.HBM)
    like = arrays[0]
    shape = jax.ShapeDtypeStruct(like.shape, F32)
    return pl.pallas_call(
        functools.partial(moments_kernel, first_part),
        in_specs=[hbm] * len(arrays),
        out_specs=[hbm] * 2,
        out_shape=[shape, shape],
        scratch_shapes=[
            pltpu.VMEM(like.shape, F32),
            pltpu.VMEM(like.shape, F32),
            pltpu.VMEM(like.shape, BF16),
            pltpu.SemaphoreType.DMA((5, E)),
        ],
        input_output_aliases={} if first_part else {3: 0, 4: 1},
        compiler_params=pltpu.CompilerParams(vmem_limit_bytes=VMEM_BYTES),
        name="moments_first" if first_part else "moments_last",
    )(*arrays)


def kernel(
    tokens,
    route_in,
    weight_in,
    gate_up,
    down,
    moment_one,
    moment_two,
    gradient,
    list_in,
    count_in,
    mixed,
    route_ref,
    weight_ref,
    list_ref,
    count_ref,
    one,
    two,
    grad,
    delta,
    tok,
    full,
    selector,
    wide,
    zsend,
    xbuf,
    gu,
    dn,
    acc,
    hid,
    mix,
    tgt,
    picks,
    far,
    via,
    near,
    held,
    came,
    own,
    r2send,
    r2recv,
    r2own,
    r3buf,
    back,
    load_sem,
    gu_sem,
    adam_sem,
    sib_send,
    sib_recv,
    z_send,
    z_recv,
    w_send,
    w_recv,
    p_send,
    p_recv,
    f_send,
    f_recv,
    y_send,
    y_recv,
    d_send,
    d_recv,
    m_send,
    m_recv,
    far_s,
    far_r,
    early_s,
    early_r,
    late_s,
    late_r,
    r2s,
    r2r,
    r3s,
    r3r,
):
    x = lax.axis_index("fsdp")
    z = lax.axis_index("expert")
    t = lax.axis_index("tensor")
    y = t // 2
    c = lax.rem(t, 2)

    def at(i, j, k, core):
        return (lax.rem(x + i, 4), lax.rem(z + k, 8), lax.rem(y + j, 4) * 2 + core)

    def along(h, i):
        return at(i * (1 - h), i * h, 0, c)

    def remote(src, dst, ssem, rsem, where):
        return pltpu.make_async_remote_copy(
            src_ref=src,
            dst_ref=dst,
            send_sem=ssem,
            recv_sem=rsem,
            device_id=where,
            device_id_type=MESH_ID,
        )

    barrier = pltpu.get_barrier_semaphore()
    sibling = at(0, 0, 0, 1 - c)
    for i in range(1, 4):
        for h in range(2):
            pl.semaphore_signal(barrier, inc=1, device_id=along(h, i), device_id_type=MESH_ID)
    for k in range(8):
        pl.semaphore_signal(
            barrier, inc=1, device_id=at(0, 0, k, 1 - c), device_id_type=MESH_ID
        )
        if k:
            pl.semaphore_signal(
                barrier, inc=1, device_id=at(0, 0, k, c), device_id_type=MESH_ID
            )

    def small(src, dst, n):
        return pltpu.make_async_copy(src, dst, load_sem.at[n])

    route_load = small(route_in, route_ref, 4)
    columns = pl.ds(pl.multiple_of((4 * x + y) * 2 * LANE, 2 * LANE), 2 * LANE)
    tok_load = small(tokens.at[c, :, columns], tok, 0)
    full_load = small(tokens.at[c], full, 1)
    small_loads = [
        small(list_in, list_ref, 6),
        small(count_in, count_ref, 7),
        small(weight_in, weight_ref, 8),
    ]
    adam_loads = [
        pltpu.make_async_copy(src, dst, adam_sem.at[n])
        for n, (src, dst) in enumerate(((moment_one, one), (moment_two, two), (gradient, grad)))
    ]
    down_load = small(down, dn.at[pl.ds(0, HS)], 2)
    for cp in [route_load, tok_load, full_load] + small_loads + adam_loads:
        cp.start()

    def gu_load(q):
        rows = pl.ds(pl.multiple_of(q * QUART, QUART), QUART)
        return pltpu.make_async_copy(
            gate_up.at[:, rows, :], gu.at[0, :, rows, :], gu_sem.at[q]
        )

    lower = (
        lax.broadcasted_iota(jnp.int32, (TOK, TOK), 0)
        < lax.broadcasted_iota(jnp.int32, (TOK, TOK), 1)
    ).astype(BF16)
    expert_ids = lax.broadcasted_iota(jnp.int32, (E, TOK), 0)
    slot_ids = lax.broadcasted_iota(jnp.int32, (CAP, TOK), 0).astype(F32)

    def slots_of(step):
        named = route_ref[step]
        hits = [named[k : k + 1, :] == expert_ids for k in range(2)]
        any_hit = jnp.where(hits[0] | hits[1], 1.0, 0.0)
        place = jnp.dot(any_hit.astype(BF16), lower, preferred_element_type=F32)
        place = jnp.where(any_hit > 0.5, place, -1.0)
        return hits, [slot_ids == place[e : e + 1, :] for e in range(E)]

    route_load.wait()
    _, chosen = slots_of(c)
    selector[...] = jnp.concatenate(
        [jnp.where(m, 1.0, 0.0) for m in chosen], axis=0
    ).astype(BF16)
    tok_load.wait()
    picked = jnp.dot(selector[...], tok[...], preferred_element_type=F32).astype(BF16)
    for h in range(2):
        zsend[h] = picked[:, h * LANE : (h + 1) * LANE]

    def expert_rows(n):
        return pl.ds(pl.multiple_of(lax.rem(z + NEAR[n], 8) * CAP, CAP), CAP)

    own_rows = expert_rows(0)

    pl.semaphore_wait(barrier, 21)

    def z_copy(n):
        return remote(
            zsend.at[:, expert_rows(n), :],
            xbuf.at[:, 0, 0, pl.ds(n * CAP, CAP), :],
            z_send.at[n],
            z_recv.at[n],
            at(0, 0, NEAR[n], c),
        )

    def wide_copy(n, h):
        return remote(
            wide.at[n - 1, h],
            xbuf.at[h, :, :, pl.ds(n * CAP, CAP), :],
            w_send.at[n, h],
            w_recv.at[n, h],
            at(0, 0, NEAR[n], c),
        )

    for n in range(7, WIDE - 1, -1):
        z_copy(n).start()

    def group(g):
        start, end = GROUPS[g]
        return pl.ds(start * CAP, (end - start) * CAP)

    def half_group(g, w):
        start, end = GROUPS[g]
        size = (end - start) * CAP // 2
        return pl.ds(start * CAP + w * size, size)

    def first_copy(h, i, g):
        rows = group(g)
        return remote(
            xbuf.at[h, 0, 0, rows, :],
            xbuf.at[h, 0, i, rows, :],
            p_send.at[h, i, g],
            p_recv.at[h, i, g],
            along(h, i),
        )

    def second_copy(h, w, i, g):
        rows = group(g)
        return remote(
            xbuf.at[h, 0, i, rows, :],
            xbuf.at[h, 1 + 2 * w, i, rows, :],
            f_send.at[h, w, i, g],
            f_recv.at[h, w, i, g],
            along(1 - h, 1 + 2 * w),
        )

    def relay(h, w, i, g):
        rows = half_group(g, w)
        return remote(
            xbuf.at[h, 1 + 2 * w, i, rows, :],
            xbuf.at[h, 2, i, rows, :],
            y_send.at[h, w, i, g],
            y_recv.at[h, w, i, g],
            along(1 - h, 1 + 2 * w),
        )

    def start_group(g):
        for n in range(*GROUPS[g]):
            z_copy(n).wait_recv()
        for i in (2, 1, 3):
            for h in range(2):
                first_copy(h, i, g).start()
        for h in range(2):
            for w in range(2):
                second_copy(h, w, 0, g).start()

    def spread(g):
        for i in (1, 3, 2):
            for h in range(2):
                first_copy(h, i, g).wait_recv()
                for w in range(2):
                    second_copy(h, w, i, g).start()

    def pass_on(i, g):
        for h in range(2):
            for w in range(2):
                second_copy(h, w, i, g).wait_recv()
                relay(h, w, i, g).start()

    def gu_swap(q):
        rows = pl.ds(pl.multiple_of(q * QUART, QUART), QUART)
        return remote(
            gate_up.at[:, rows, :],
            gu.at[1, :, rows, :],
            sib_send.at[q],
            sib_recv.at[q],
            sibling,
        )

    @pl.loop(0, 8)
    def _(q):
        gu_load(q).start()
        gu_swap(q).start()

    down_swap = remote(
        down, dn.at[pl.ds(HS, HS)], m_send.at[0], m_recv.at[0], sibling
    )
    down_swap.start()
    down_load.start()

    for cp in small_loads:
        cp.wait()
    here = lax.broadcasted_iota(jnp.int32, (MAXCH, E), 1) == z
    blocks = jnp.sum(jnp.where(here, list_ref[...], 0), axis=1, keepdims=True)
    count = jnp.sum(jnp.where(here[0:1], count_ref[...], 0), axis=1, keepdims=True)
    lane = lax.broadcasted_iota(jnp.int32, (8, LANE), 1)

    def targets(first_lane, first_unit):
        units = jnp.full((8, LANE), -1, jnp.int32)
        for j in range(MAXCH):
            start = first_lane + BLOCK_ROWS * j
            live = (lane >= start) & (lane < start + BLOCK_ROWS) & (count > j)
            unit = first_unit + 4 * (BLOCK_ROWS * blocks[j : j + 1, :] + lane - start)
            units = jnp.where(live, unit, units)
        return units.astype(F32)

    tgt[0] = targets(0, 0)
    tgt[1] = targets(CAP, HS)
    target_swap = remote(tgt.at[1], tgt.at[2], m_send.at[1], m_recv.at[1], sibling)
    target_swap.start()
    dn[pl.ds(2 * HS + 2 * CAP, 2 * CAP), :] = jnp.zeros((2 * CAP, D), BF16)

    row_ids = lax.broadcasted_iota(jnp.int32, (BLOCK_ROWS, 2 * CAP), 0)
    unit_ids = lax.broadcasted_iota(jnp.int32, (BLOCK_ROWS, 2 * CAP), 1)
    expert_lane = lax.broadcasted_iota(jnp.int32, (MAXCH, E), 1)

    def adam(e):
        wide = grad[e].astype(F32)
        top = BETA_ONE * one[e] + (1.0 - BETA_ONE) * wide
        bottom = BETA_TWO * two[e] + (1.0 - BETA_TWO) * wide * wide
        steps = -(LEARN_RATE * (top / FIRST_FIX) / (jnp.sqrt(bottom / SECOND_FIX) + ADAM_EPS))
        numbers = jnp.sum(
            jnp.where(expert_lane == e, list_ref[...], 0), axis=1, keepdims=True
        )
        taken = [
            jnp.where(unit_ids == BLOCK_ROWS * numbers[j : j + 1, :] + row_ids, 1.0, 0.0)
            for j in range(MAXCH)
        ]
        delta[e] = jnp.dot(
            jnp.concatenate(taken, axis=0).astype(BF16),
            steps.astype(BF16),
            preferred_element_type=F32,
        ).astype(BF16)

    for cp in adam_loads:
        cp.wait()

    @pl.loop(0, 4)
    def _(e):
        adam(e)

    start_group(0)

    @pl.loop(4, 8)
    def _(e):
        adam(e)

    delta_cols = pl.ds(pl.multiple_of(z * QUART, QUART), QUART)

    def d_copy(k):
        e = lax.rem(z + k, 8)
        return remote(
            delta.at[e],
            dn.at[pl.ds(2 * HS, CAP), delta_cols],
            d_send.at[k],
            d_recv.at[k],
            at(0, 0, k, c),
        )

    @pl.loop(1, 8)
    def _(k):
        d_copy(k).start()

    dn[pl.ds(2 * HS, CAP), delta_cols] = delta[z]
    start_group(1)

    full_load.wait()

    @pl.loop(0, 8)
    def _(q):
        h, j = q // 4, lax.rem(q, 4)
        parts = []
        for i in range(4):
            a, b = i + h * (j - i), j + h * (i - j)
            chip = 4 * lax.rem(x - a + 4, 4) + lax.rem(y - b + 4, 4)
            start = pl.multiple_of(chip * 2 * LANE + h * LANE, LANE)
            parts.append(full[:, pl.ds(start, LANE)])
        block = jnp.concatenate(parts, axis=1)
        for n in range(WIDE):
            rows = jnp.dot(
                selector[expert_rows(n), :], block, preferred_element_type=F32
            ).astype(BF16)
            for i in range(4):
                piece = rows[:, i * LANE : (i + 1) * LANE]
                if n:
                    wide[n - 1, h, j, i] = piece
                else:
                    xbuf[h, j, i, pl.ds(0, CAP), :] = piece

    for n in range(1, WIDE):
        for h in range(2):
            wide_copy(n, h).start()


    spread(0)
    pass_on(0, 0)
    spread(1)
    pass_on(0, 1)

    def project(h, j, first):
        block = jnp.concatenate([xbuf[h, j, i] for i in range(4)], axis=1)
        for s in range(2):
            for g in range(2):
                parts = []
                for i in range(4):
                    a, b = i + h * (j - i), j + h * (i - j)
                    chip = 4 * lax.rem(x - a + 4, 4) + lax.rem(y - b + 4, 4)
                    rows = pl.ds(pl.multiple_of(chip * 2 * LANE + h * LANE, LANE), LANE)
                    parts.append(gu[s, g, rows, :])
                term = jnp.dot(
                    block, jnp.concatenate(parts, axis=0), preferred_element_type=F32
                )
                if first:
                    acc[2 * s + g] = term
                else:
                    acc[2 * s + g] += term

    @pl.loop(0, 8)
    def _(q):
        gu_load(q).wait()
        gu_swap(q).wait_recv()

    for g in range(2):
        for i in (1, 3, 2):
            pass_on(i, g)
    for n in range(1, WIDE):
        for h in range(2):
            wide_copy(n, h).wait_recv()
    project(0, 0, True)
    project(1, 0, False)

    for k in range(1, 8):
        d_copy(k).wait_recv()
    delta_swap = remote(
        dn.at[pl.ds(2 * HS, CAP)],
        dn.at[pl.ds(2 * HS + CAP, CAP)],
        m_send.at[2],
        m_recv.at[2],
        sibling,
    )
    delta_swap.start()

    target_swap.wait_recv()
    unit = jnp.where(lane < CAP, tgt[0], tgt[2])[0:1, :]
    picks[...] = (
        lax.broadcasted_iota(jnp.int32, (2 * HS, LANE), 0).astype(F32) == unit
    ).astype(BF16)

    for step in range(2):
        hits, chosen = slots_of(step)
        w = weight_ref[step]
        by_expert = jnp.where(hits[0], w[0:1, :], 0.0) + jnp.where(hits[1], w[1:2, :], 0.0)
        full = jnp.concatenate(
            [jnp.where(chosen[e], by_expert[e : e + 1, :], 0.0) for e in range(E)], axis=0
        )
        full = full.T
        high = full.astype(BF16)
        mix[step, pl.ds(0, TOK), :] = high
        mix[step, pl.ds(TOK, TOK), :] = (full - high.astype(F32)).astype(BF16)

    @pl.loop(0, 4)
    def _(q):
        project(lax.rem(q, 2), 1 + 2 * (q // 2), False)

    for h in range(2):
        for i in range(4):
            for g in range(2):
                for w in range(2):
                    relay(h, w, i, g).wait_recv()
        project(h, 2, False)

    for s in range(2):
        gate = acc[2 * s]
        hid[:, pl.ds(s * HS, HS)] = (jax.nn.silu(gate) * acc[2 * s + 1]).astype(BF16)
    hid[:, pl.ds(2 * HS, LANE)] = jnp.dot(
        hid[:, pl.ds(0, 2 * HS)], picks[...], preferred_element_type=F32
    ).astype(BF16)

    down_load.wait()
    down_swap.wait_recv()
    delta_swap.wait_recv()

    def down_term(h, i):
        cols = []
        for j in range(4):
            a, b = i + h * (j - i), j + h * (i - j)
            block = 8 * lax.rem(x + a, 4) + 2 * lax.rem(y + b, 4) + h
            cols.append(dn[:, pl.ds(pl.multiple_of(block * LANE, LANE), LANE)])
        return jnp.dot(hid[...], jnp.concatenate(cols, axis=1), preferred_element_type=F32)

    def far_copy(h, w, b):
        return remote(
            far.at[h, pl.ds(w * HALF + (1 - b) * QROWS, QROWS), :],
            via.at[h, w, pl.ds((1 - b) * QROWS, QROWS), :],
            far_s.at[h, w, b],
            far_r.at[h, w, b],
            along(h, 1 + 2 * w),
        )

    def early_copy(h, w):
        rows = pl.ds((1 - w) * HALF, HALF)
        return remote(
            near.at[h, w, rows, :],
            came.at[h, w, rows, :],
            early_s.at[h, w],
            early_r.at[h, w],
            along(h, 1 + 2 * w),
        )

    def late_copy(h, w, b):
        rows = pl.ds(w * HALF + (1 - b) * QROWS, QROWS)
        return remote(
            near.at[h, w, rows, :],
            came.at[h, w, rows, :],
            late_s.at[h, w, b],
            late_r.at[h, w, b],
            along(h, 1 + 2 * w),
        )

    @pl.loop(0, 2)
    def _(h):
        far[h] = down_term(h, 2).astype(BF16)
        for b in range(2):
            for w in range(2):
                far_copy(h, w, b).start()

    for w in range(2):

        @pl.loop(0, 2)
        def _(h):
            term = down_term(h, 1 + 2 * w)
            direct = (1 - w) * HALF
            near[h, w, pl.ds(direct, HALF), :] = term[direct : direct + HALF].astype(BF16)
            early_copy(h, w).start()
            held[h, w] = term[w * HALF : (w + 1) * HALF]

    for b in range(2):
        rows = pl.ds((1 - b) * QROWS, QROWS)
        for h in range(2):
            for w in range(2):
                far_copy(h, w, b).wait_recv()
                near[h, w, pl.ds(w * HALF + (1 - b) * QROWS, QROWS), :] = (
                    held[h, w, rows, :] + via[h, w, rows, :].astype(F32)
                ).astype(BF16)
                late_copy(h, w, b).start()

    @pl.loop(0, 2)
    def _(h):
        own[h] = down_term(h, 0)

    for n in range(WIDE, 8):
        z_copy(n).wait_send()
    for n in range(1, WIDE):
        for h in range(2):
            wide_copy(n, h).wait_send()
    for h in range(2):
        for g in range(2):
            for i in range(4):
                if i:
                    first_copy(h, i, g).wait_send()
                for w in range(2):
                    second_copy(h, w, i, g).wait_send()
                    relay(h, w, i, g).wait_send()

    @pl.loop(0, 8)
    def _(q):
        gu_swap(q).wait_send()

    for k in range(1, 8):
        d_copy(k).wait_send()
    for cp in (down_swap, target_swap, delta_swap):
        cp.wait_send()

    def r2_copy(h, j, b):
        return remote(
            r2send.at[h, j - 1, b],
            r2recv.at[h, j - 1, b],
            r2s.at[h, j - 1, b],
            r2r.at[h, j - 1, b],
            along(1 - h, j),
        )

    for b in range(2):
        for h in range(2):
            for w in range(2):
                if b == 0:
                    early_copy(h, w).wait_recv()
                late_copy(h, w, b).wait_recv()
            for m in range(2):
                rows = pl.ds(m * HALF + (1 - b) * QROWS, QROWS)
                put = pl.ds(m * QROWS, QROWS)
                for j in (2, 1, 3, 0):
                    cols = pl.ds(j * LANE, LANE)
                    total = (
                        own[h, rows, cols]
                        + came[h, 0, rows, cols].astype(F32)
                        + came[h, 1, rows, cols].astype(F32)
                    )
                    if j:
                        r2send[h, j - 1, b, put, :] = total.astype(BF16)
                    else:
                        r2own[h, b, put, :] = total
            for j in (2, 1, 3):
                r2_copy(h, j, b).start()

    for h in range(2):
        for w in range(2):
            early_copy(h, w).wait_send()
            for b in range(2):
                far_copy(h, w, b).wait_send()
                late_copy(h, w, b).wait_send()

    def r3_rows(n):
        return 1 - (n // 2) % 2, pl.ds((n % 2) * CAP + (n // 4) * QROWS, CAP)

    def r3_copy(h, n):
        b, rows = r3_rows(n)
        return remote(
            r3buf.at[h, b, rows, :],
            back.at[c, own_rows, :],
            r3s.at[n, h],
            r3r.at[n, c],
            at(0, 0, 8 - NEAR[n], h),
        )

    def r3_wait(step, n):
        rows = pl.ds(pl.multiple_of(lax.rem(z + NEAR[n], 8) * CAP, CAP), CAP)
        remote(
            back.at[step, rows, :],
            back.at[step, rows, :],
            r3s.at[n, step],
            r3r.at[n, step],
            at(0, 0, NEAR[n], step),
        ).wait_recv()

    for b in range(2):
        for h in range(2):
            for j in (1, 3, 2):
                r2_copy(h, j, b).wait_recv()
            total = r2own[h, b]
            for j in range(3):
                total += r2recv[h, j, b].astype(F32)
            r3buf[h, b] = total.astype(BF16)
            for n in (7, 6, 3, 2) if b == 0 else (5, 4, 1):
                r3_copy(h, n).start()
    r3_copy(1 - c, 0).start()
    b, rows = r3_rows(0)
    back[c, own_rows, :] = r3buf[c, b, rows, :]
    for h in range(2):
        for j in range(1, 4):
            for b in range(2):
                r2_copy(h, j, b).wait_send()
    r3_wait(1 - c, 0)
    for step in range(2):
        for n in range(1, 8):
            r3_wait(step, n)
        both = jnp.dot(mix[step], back[step], preferred_element_type=F32)
        mixed[step] = (both[:TOK] + both[TOK:]).astype(BF16)

    r3_copy(1 - c, 0).wait_send()
    for n in range(1, 8):
        for h in range(2):
            r3_copy(h, n).wait_send()


def experts(*args):
    hbm = pl.BlockSpec(memory_space=pltpu.HBM)
    dma = pltpu.SemaphoreType.DMA
    rows, cols = args[5].shape[1:]
    return pl.pallas_call(
        kernel,
        in_specs=[hbm] * 10,
        out_specs=pl.BlockSpec(memory_space=pltpu.VMEM),
        out_shape=pltpu.VMEM((2, TOK, LANE), BF16),
        scratch_shapes=[
            pltpu.VMEM((2, 2, TOK), jnp.int32),
            pltpu.VMEM((2, 2, TOK), F32),
            pltpu.VMEM((MAXCH, E), jnp.int32),
            pltpu.VMEM((1, E), jnp.int32),
            pltpu.VMEM((E, rows, cols), F32),
            pltpu.VMEM((E, rows, cols), F32),
            pltpu.VMEM((E, rows, cols), BF16),
            pltpu.VMEM((E, CAP, cols), BF16),
            pltpu.VMEM((TOK, 2 * LANE), BF16),
            pltpu.VMEM((TOK, D), BF16),
            pltpu.VMEM((SLOTS, TOK), BF16),
            pltpu.VMEM((2, 2, 4, 4, CAP, LANE), BF16),
            pltpu.VMEM((2, SLOTS, LANE), BF16),
            pltpu.VMEM((2, 4, 4, SLOTS, LANE), BF16),
            pltpu.VMEM((2, 2, D, HS), BF16),
            pltpu.VMEM((KDOWN, D), BF16),
            pltpu.VMEM((4, SLOTS, HS), F32),
            pltpu.VMEM((SLOTS, KDOWN), BF16),
            pltpu.VMEM((2, 2 * TOK, SLOTS), BF16),
            pltpu.VMEM((3, 8, LANE), F32),
            pltpu.VMEM((2 * HS, LANE), BF16),
            pltpu.VMEM((2, SLOTS, QUART), BF16),
            pltpu.VMEM((2, 2, HALF, QUART), BF16),
            pltpu.VMEM((2, 2, SLOTS, QUART), BF16),
            pltpu.VMEM((2, 2, HALF, QUART), F32),
            pltpu.VMEM((2, 2, SLOTS, QUART), BF16),
            pltpu.VMEM((2, SLOTS, QUART), F32),
            pltpu.VMEM((2, 3, 2, HALF, LANE), BF16),
            pltpu.VMEM((2, 3, 2, HALF, LANE), BF16),
            pltpu.VMEM((2, 2, HALF, LANE), F32),
            pltpu.VMEM((2, 2, HALF, LANE), BF16),
            pltpu.VMEM((2, SLOTS, LANE), BF16),
            dma((9,)),
            dma((8,)),
            dma((3,)),
            dma((8,)),
            dma((8,)),
            dma((8,)),
            dma((8,)),
            dma((3, 2)),
            dma((3, 2)),
            dma((2, 4, 2)),
            dma((2, 4, 2)),
            dma((2, 2, 4, 2)),
            dma((2, 2, 4, 2)),
            dma((2, 2, 4, 2)),
            dma((2, 2, 4, 2)),
            dma((8,)),
            dma((8,)),
            dma((3,)),
            dma((3,)),
            dma((2, 2, 2)),
            dma((2, 2, 2)),
            dma((2, 2)),
            dma((2, 2)),
            dma((2, 2, 2)),
            dma((2, 2, 2)),
            dma((2, 3, 2)),
            dma((2, 3, 2)),
            dma((8, 2)),
            dma((8, 2)),
        ],
        compiler_params=pltpu.CompilerParams(
            collective_id=1, has_side_effects=True, vmem_limit_bytes=VMEM_BYTES
        ),
        cost_estimate=pl.CostEstimate(
            flops=3_600_000_000, bytes_accessed=12_000_000, transcendentals=400_000
        ),
        name="experts",
    )(*args)


def on_device(
    tokens,
    route,
    route_weight,
    gate_up,
    down_weight,
    adam_first,
    adam_second,
    gradient,
    block_list,
    block_count,
):
    inputs = (adam_first, adam_second, gradient)
    made = moments(True, *inputs)
    *made, tokens = lax.optimization_barrier((*made, tokens))
    mixed = experts(
        tokens,
        route.transpose(0, 2, 1),
        route_weight.transpose(0, 2, 1),
        gate_up[0],
        down_weight[0],
        adam_first,
        adam_second,
        gradient,
        block_list[:, 0, :].T,
        block_count.T,
    )
    *made, mixed = lax.optimization_barrier((*made, mixed))
    return mixed, *moments(False, *inputs, *made)


def solution(mesh):
    return jax.shard_map(
        on_device,
        mesh=mesh,
        in_specs=(
            P(None, "expert", None),
            P(None, "expert", None),
            P(None, "expert", None),
            P("expert", None, None, ("fsdp", "tensor")),
            P("expert", ("fsdp", "tensor"), None),
            P(None, ("fsdp", "tensor"), "expert"),
            P(None, ("fsdp", "tensor"), "expert"),
            P(None, ("fsdp", "tensor"), "expert"),
            P(None, ("fsdp", "tensor"), None),
            P(None, ("fsdp", "tensor")),
        ),
        out_specs=(
            P(None, "expert", ("fsdp", "tensor")),
            P(None, ("fsdp", "tensor"), "expert"),
            P(None, ("fsdp", "tensor"), "expert"),
        ),
        check_vma=False,
    )
```
